512 devices in a mesh: tm: 128 (over z, y, core), lev: 4 (over x).
Axes of the slice: x: 4, y: 4, z: 16, core: 2. Of those that a mesh axis runs over, the one named last changes fastest.
Arguments:
- field: bfloat16 [256, 4, 384, 384], P('tm', 'lev'), may hold values from -6 to 6
- patch_list: int32 [128, 128, 2], P('tm'), may hold values from -1 to 31, as said below
- track_time: int32 [4096], replicated, may hold values from 0 to 255
- track_row: int32 [4096], replicated, may hold values from 64 to 320
- track_col: int32 [4096], replicated, may hold values from 64 to 320
Outputs:
- point_fields: bfloat16 [4096, 4, 512], P('tm', 'lev')
- composite: float32 [4, 512], P('lev')
- covariance: float32 [128, 128], P('lev')
The draws below stay inside these ranges and needn't reach their ends.
Inputs may be any that keep to these rules, and one draw needn't show every extreme that they name: For each owner d, each k appears at most once in patch_list[:, d, :]; where patch_list[s, d, c] = k >= 0, track_time[d * 32 + k] lies in group s, that is from s * 2 to (s + 1) * 2 - 1; some group fills all 2 slots to some owner.
All inputs are finite; a program needn't handle non-finite values.
Results may differ from the reference program's by a relative error of at most 0.001.
Values may be sent and summed in bfloat16 or wider, within the bound.
A program may use at most 64 MiB of HBM per device.

```python
import math
import jax
import jax.numpy as jnp
from jax import lax

PATCH = 128
NR = 32
NA = 16
T_DEV = 2
P_DEV = 32
H = 384
W = 384
SLOT_LIMIT = 2
LEVELS = 4
TIMES = 256
POINTS = 4096
F = 128
N_TM = 128


def draw_field(key, part):
    base = jax.random.fold_in(key, 7004)
    shared_key = jax.random.fold_in(base, 1)
    level_key = jax.random.fold_in(base, 2)
    shared = jnp.clip(jax.random.normal(shared_key, (TIMES, 1, H, W), jnp.float32), -4.0, 4.0)
    own = jnp.clip(jax.random.normal(level_key, (TIMES, LEVELS, H, W), jnp.float32), -4.0, 4.0)
    values = 0.8 * shared + 0.6 * own
    return values.astype(jnp.bfloat16)


def track_layout(key):
    base = jax.random.fold_in(key, 7001)
    busy = jax.random.randint(jax.random.fold_in(base, 1), (N_TM,), 0, 4)
    noise = jax.random.randint(jax.random.fold_in(base, 2), (N_TM, N_TM * SLOT_LIMIT), 0, 2 ** 18)
    slot_source = jnp.arange(N_TM * SLOT_LIMIT, dtype=jnp.int32) // SLOT_LIMIT
    rating_value = busy[slot_source][None, :] * 2 ** 16 + noise
    final_slot = N_TM * SLOT_LIMIT - 1
    extra_credit = jnp.zeros((N_TM, N_TM * SLOT_LIMIT), jnp.int32)
    extra_credit = extra_credit.at[0, 0].set(2 ** 20).at[0, final_slot].set(2 ** 20)
    rating_value = rating_value + extra_credit
    order = jnp.argsort(-rating_value, axis=1, stable=True)[:, :P_DEV].astype(jnp.int32)
    keep = jax.random.randint(jax.random.fold_in(base, 3), (N_TM, P_DEV), 0, 8) != 0
    local = jnp.where(keep, jnp.arange(P_DEV, dtype=jnp.int32)[None, :], -1)
    table = jnp.full((N_TM, N_TM * SLOT_LIMIT), -1, jnp.int32)
    table = table.at[jnp.arange(N_TM, dtype=jnp.int32)[:, None], order].set(local)
    patch_list = table.reshape(N_TM, N_TM, SLOT_LIMIT).transpose(1, 0, 2)
    source = order // SLOT_LIMIT
    offset = jax.random.randint(jax.random.fold_in(base, 4), (N_TM, P_DEV), 0, T_DEV)
    first_owner = jnp.arange(N_TM, dtype=jnp.int32)[:, None] == 0
    offset = jnp.where(first_owner & (order == final_slot), T_DEV - 1, offset)
    offset = jnp.where(first_owner & (order == 0), 0, offset)
    track_time = (source * T_DEV + offset).reshape(-1)
    return (patch_list.astype(jnp.int32), track_time.astype(jnp.int32))


def draw_patch_list(key, part):
    return track_layout(key)[0]


def draw_track_time(key, part):
    return track_layout(key)[1]


def draw_track_row(key, part):
    return jax.random.randint(jax.random.fold_in(key, 7002), (POINTS,), PATCH // 2, H - PATCH // 2 + 1).astype(jnp.int32)


def draw_track_col(key, part):
    return jax.random.randint(jax.random.fold_in(key, 7003), (POINTS,), PATCH // 2, W - PATCH // 2 + 1).astype(jnp.int32)


def setup_inputs(seed: int = 0) -> dict:
    splits = jax.random.split(jax.random.key(seed), 6)
    return {
        "field": draw_field(jax.random.fold_in(splits[5], 71), 0),
        "patch_list": draw_patch_list(jax.random.fold_in(splits[5], 71), 0),
        "track_time": draw_track_time(jax.random.fold_in(splits[5], 71), 0),
        "track_row": draw_track_row(jax.random.fold_in(splits[5], 71), 0),
        "track_col": draw_track_col(jax.random.fold_in(splits[5], 71), 0),
    }


def polar_offsets(patch, radii, azimuths):
    cycle = jnp.arange(radii, dtype=jnp.float32)
    turn = jnp.arange(azimuths, dtype=jnp.float32)
    radius = (cycle[:, None] + 1.0) * (5.0 * patch / (16.0 * radii))
    theta = turn[None, :] * (2.0 * math.pi / azimuths)
    across = (radius * jnp.cos(theta)).reshape(-1)
    along = (radius * jnp.sin(theta)).reshape(-1)
    return across, along


def reference(field, patch_list, track_time, track_row, track_col):
    half = PATCH // 2
    height = field.shape[2]
    local = jnp.arange(P_DEV, dtype=jnp.int32)
    hits = jnp.any(patch_list[:, :, :, None] == local, axis=(0, 2))
    live = hits.reshape(-1)
    across, along = polar_offsets(PATCH, NR, NA)
    row_pos = 0.5 * PATCH + along
    row_low = jnp.floor(row_pos)
    row_frac = row_pos - row_low
    row_low = row_low.astype(jnp.int32)
    upper_w = row_frac.astype(jnp.bfloat16).astype(jnp.float32)
    lower_w = (1.0 - row_frac).astype(jnp.bfloat16).astype(jnp.float32)
    zero = jnp.zeros((), jnp.int32)

    def single_point(index):
        time_index = track_time[index].astype(jnp.int32)
        row = track_row[index].astype(jnp.int32)
        col = track_col[index].astype(jnp.int32)
        frame = lax.dynamic_slice(field, (time_index, zero, row - half, col - half), (1, LEVELS, PATCH, PATCH))[0].astype(jnp.float32)
        latitude = 0.25 * (0.5 * (height - 1) - row.astype(jnp.float32))
        coslat = jnp.cos(latitude * (math.pi / 180.0))
        col_pos = 0.5 * PATCH + across / coslat
        col_low = jnp.floor(col_pos)
        col_frac = col_pos - col_low
        col_low = col_low.astype(jnp.int32)
        left = lower_w * frame[:, row_low, col_low] + upper_w * frame[:, row_low + 1, col_low]
        right = lower_w * frame[:, row_low, col_low + 1] + upper_w * frame[:, row_low + 1, col_low + 1]
        return (1.0 - col_frac) * left + col_frac * right

    polar = lax.map(single_point, jnp.arange(POINTS, dtype=jnp.int32))
    polar = jnp.where(live[:, None, None], polar, jnp.zeros((), jnp.float32))
    count = jnp.sum(live.astype(jnp.float32))
    composite = jnp.sum(polar, axis=0) / count
    profile = jnp.mean(polar.reshape(POINTS, LEVELS, NR, NA), axis=-1).reshape(POINTS, F)
    mean_all = jnp.sum(profile, axis=0) / count
    gram = jnp.dot(profile.T, profile, precision=lax.Precision.HIGHEST, preferred_element_type=jnp.float32)
    covariance = gram / count - mean_all[:, None] * mean_all[None, :]
    return polar.astype(jnp.bfloat16), composite, covariance
```

```python
import functools
import math

import jax
import jax.numpy as jnp
import numpy as np
from jax import lax
from jax.experimental import pallas as pl
from jax.experimental.pallas import tpu as pltpu
from jax.sharding import PartitionSpec as P

PATCH, NR, NA = 128, 32, 16
HALF = PATCH // 2
SIZE = 384
POINTS_DEV = 32
OWNERS, SLOTS = 128, 2
PLANES, MATES, LEVS = 16, 8, 4
SPAN = 64
TILES = ((0, 6), (4, 8), (0, 3), (1, 8))
GROUPS = 4
CHUNKS = 5


def tables():
    with jax.ensure_compile_time_eval():
        cycle = jnp.arange(NR, dtype=jnp.float32)
        turn = jnp.arange(NA, dtype=jnp.float32)
        radius = (cycle[:, None] + 1.0) * (5.0 * PATCH / (16.0 * NR))
        theta = turn[None, :] * (2.0 * math.pi / NA)
        across = np.asarray((radius * jnp.cos(theta)).reshape(-1))
        along = (radius * jnp.sin(theta)).reshape(-1)
        pos = 0.5 * PATCH + along
        low = jnp.floor(pos)
        frac = pos - low
        upper = np.asarray(frac.astype(jnp.bfloat16)).astype(np.float32)
        lower = np.asarray((1.0 - frac).astype(jnp.bfloat16)).astype(np.float32)
        low = np.asarray(low.astype(jnp.int32))
        latitude = 0.25 * (0.5 * (SIZE - 1) - jnp.arange(SIZE, dtype=jnp.float32))
        stretch = np.asarray(1.0 / jnp.cos(latitude * (math.pi / 180.0)))
    turns = np.arange(NR * NA) % NA
    key = np.where(turns == NA // 4, -1e-3, np.where(turns == 3 * NA // 4, 1e-3, across))
    order = np.argsort(key, kind="stable")
    q = np.arange(NR * NA)
    weights = np.zeros((PATCH, NR * NA), np.float32)
    weights[low[order], q] += lower[order]
    weights[low[order] + 1, q] += upper[order]
    mean = np.zeros((4, NR, 128), np.float32)
    mean[q // 128, order // NA, q % 128] = 1.0 / NA
    unsort = np.zeros((NR * NA, NR * NA), np.float32)
    unsort[q, order] = 1.0
    spread = np.ascontiguousarray(np.broadcast_to(across[order].reshape(4, 1, 128), (4, 8, 128)), np.float32)
    return stretch, weights.astype(jnp.bfloat16), spread, mean, unsort.astype(jnp.bfloat16)


def merge(a, b, step, mask):
    if step == 4:
        return jnp.where(mask, a, b) + pltpu.roll(jnp.where(mask, b, a), 4, 0)
    return jnp.where(mask, a + pltpu.roll(a, 8 - step, 0), b + pltpu.roll(b, step, 0))


def regrid_kernel(
    list_ref, time_ref, row_ref, col_ref, stretch_ref, field_ref, weights_ref, across_ref, mean_ref,
    send_ref, prof_ref, sums_ref, turned, polar,
):
    here = lax.axis_index("tm")
    for t in range(2):
        for i in range(3):
            for j in range(3):
                tile = field_ref[t, 0, i * 128 : (i + 1) * 128, j * 128 : (j + 1) * 128]
                turned[t, i, j * 128 : (j + 1) * 128, :] = tile.astype(jnp.float32).T
    sub = lax.broadcasted_iota(jnp.int32, (8, 128), 0)
    first = (lax.broadcasted_iota(jnp.int32, (8, 128), 1) & 4) == 0
    lane = lax.broadcasted_iota(jnp.int32, (SPAN, 128), 1)
    subf = sub.astype(jnp.float32)
    m4, m2, m1 = sub < 4, (sub & 2) == 0, (sub & 1) == 0

    def plane(g, carry):
        total, count = carry
        halves, info = ([], []), []
        names = jnp.zeros((8, 128), jnp.int32)
        for o in range(MATES):
            owner = g * MATES + o
            ids = []
            for p in range(SLOTS):
                k = list_ref[owner * SLOTS + p]
                ids.append(k)
                point = owner * POINTS_DEV + jnp.maximum(k, 0)
                t = jnp.clip(time_ref[point] - 2 * here, 0, 1)
                row, col = row_ref[point], col_ref[point]
                top = row - HALF
                b = jnp.minimum(top // 128, 1)
                off = top - b * 128
                starts = [pl.multiple_of((col - reach) // 8 * 8, 8) for reach in (48, 1)]
                for h in range(2):
                    one = turned[t, b, pl.ds(starts[h], SPAN), :]
                    two = turned[t, b + 1, pl.ds(starts[h], SPAN), :]
                    both = jnp.where(lane >= off, one, two)
                    halves[h].append(pltpu.roll(both, 128 - off, 1).astype(jnp.bfloat16))
                live = jnp.where(k >= 0, 1.0, 0.0)
                count += live
                info.append((stretch_ref[row], [(col - s).astype(jnp.float32) for s in starts], live))
            names = jnp.where(sub == o, jnp.where(first, ids[0], ids[1]), names)
        mixed = [
            jnp.dot(
                jnp.concatenate(halves[h], 0),
                weights_ref[:, h * 256 : (h + 1) * 256],
                preferred_element_type=jnp.float32,
            )
            for h in range(2)
        ]
        for o in range(MATES):
            accs = []
            for n in (2 * o, 2 * o + 1):
                s, centre, _ = info[n]
                for blk in range(4):
                    base = across_ref[blk] * s + (centre[blk // 2] - subf)
                    acc = None
                    for tile in range(*TILES[blk]):
                        w = jnp.maximum(1.0 - jnp.abs(base - 8.0 * tile), 0.0)
                        at = n * SPAN + tile * 8
                        v = mixed[blk // 2][at : at + 8, (blk % 2) * 128 : (blk % 2 + 1) * 128]
                        acc = w * v if acc is None else acc + w * v
                    accs.append(acc)
            a = [accs[i] for i in (0, 4, 2, 6, 1, 5, 3, 7)]
            a = [merge(a[i], a[i + 1], 4, m4) for i in (0, 2, 4, 6)]
            a = [merge(a[i], a[i + 1], 2, m2) for i in (0, 2)]
            out = merge(a[0], a[1], 1, m1) * jnp.where(m4, info[2 * o][2], info[2 * o + 1][2])
            polar[pl.ds(pl.multiple_of((g * MATES + o) * 8, 8), 8), :] = out
            send_ref[g, o] = out.astype(jnp.bfloat16)
            total = total + out
        send_ref[g, MATES] = names.astype(jnp.float32).astype(jnp.bfloat16)
        return total, count

    total, count = lax.fori_loop(0, PLANES, plane, (jnp.zeros((8, 128), jnp.float32), 0.0))
    sums_ref[...] = jnp.where(m4, jnp.where(sub == 1, count, 0.0), total + pltpu.roll(total, 4, 0))
    acc = jnp.zeros((NR, OWNERS * SLOTS), jnp.float32)
    for b in range(4):
        acc += lax.dot_general(
            mean_ref[b], polar[pl.ds(b, OWNERS * SLOTS, stride=4), :], (((1,), (1,)), ((), ())),
            precision=lax.Precision.HIGHEST, preferred_element_type=jnp.float32,
        )
    prof_ref[...] = acc


def exchange_kernel(
    send_ref, prof_ref, sums_ref, unsort_ref, out_ref, comp_ref, cov_ref,
    planes, mates, names, named, profs, part, red1, red2, red3, mine,
    plane_s, plane_r, mate_s, mate_r, name_s, name_r, prof_s, prof_r, r1_s, r1_r, r2_s, r2_r, r3_s, r3_r,
):
    tm, lev = lax.axis_index("tm"), lax.axis_index("lev")
    z, yc = tm // MATES, lax.rem(tm, MATES)
    PER = PLANES // GROUPS

    def plane_peer(d):
        return {"tm": lax.rem(z + d, PLANES) * MATES + yc}

    def mate_peer(d):
        return {"tm": z * MATES + lax.rem(yc + d, MATES)}

    def lev_peer(d):
        return {"lev": lax.rem(lev + d, LEVS)}

    def copy(src, dst, s, r, peer):
        return pltpu.make_async_remote_copy(
            src_ref=src, dst_ref=dst, send_sem=s, recv_sem=r, device_id=peer, device_id_type=pl.DeviceIdType.MESH
        )

    def each(n, f):
        def step(i, c):
            f(i)
            return c

        lax.fori_loop(1, n, step, 0)

    barrier = pltpu.get_barrier_semaphore()

    def greet(peer):
        pl.semaphore_signal(barrier, inc=1, device_id=peer, device_id_type=pl.DeviceIdType.MESH)

    each(LEVS, lambda d: greet(lev_peer(d)))
    each(MATES, lambda d: greet(mate_peer(d)))
    each(PLANES, lambda d: greet(plane_peer(d)))
    pl.semaphore_wait(barrier, LEVS + MATES + PLANES - 3)

    def prof_copy(d):
        return copy(prof_ref, profs.at[d], prof_s.at[d], prof_r.at[d], lev_peer(d))

    def plane_copy(d):
        there = lax.rem(z + d, PLANES)
        return copy(send_ref.at[there], planes.at[d], plane_s.at[d], plane_r.at[d], plane_peer(d))

    def mate_copy(g, d):
        there = lax.rem(yc + d, MATES)
        return copy(
            planes.at[pl.ds(g * PER, PER), there], mates.at[d, pl.ds(g * PER, PER)],
            mate_s.at[g, d], mate_r.at[g, d], mate_peer(d),
        )

    def name_copy(d):
        return copy(names, named.at[d], name_s.at[d], name_r.at[d], mate_peer(d))

    each(LEVS, lambda d: prof_copy(d).start())
    each(PLANES, lambda d: plane_copy(d).start())
    planes[0] = send_ref[z]
    profs[0] = prof_ref[...]

    each(LEVS, lambda d: prof_copy(d).wait_recv())
    whole = jnp.concatenate([profs[lax.rem(lev - l + LEVS, LEVS)] for l in range(LEVS)], 0)
    both = lax.dot_general(
        jnp.concatenate([prof_ref[...], jnp.ones((8, OWNERS * SLOTS), jnp.float32)], 0), whole, (((1,), (1,)), ((), ())),
        precision=lax.Precision.HIGHEST, preferred_element_type=jnp.float32,
    )
    for c in range(4):
        part[c] = both[c * 8 : (c + 1) * 8]
    sub = lax.broadcasted_iota(jnp.int32, (8, 128), 0)
    part[4] = jnp.where(sub == 0, both[32:40], sums_ref[...])

    def r1_copy(c):
        d = lax.rem(c - yc + MATES, MATES)
        return copy(part.at[c], red1.at[d], r1_s.at[c], r1_r.at[d], {"tm": z * MATES + c})

    def r2_copy(d):
        return copy(mine.at[0], red2.at[d], r2_s.at[d], r2_r.at[d], plane_peer(d))

    def r3_copy(d):
        return copy(mine.at[1], red3.at[yc], r3_s.at[d], r3_r.at[yc], mate_peer(d))

    def r1_each(f):
        for c in range(CHUNKS):
            @pl.when(yc != c)
            def _():
                f(c)

    def pass_on(g):
        for d in range(g * PER, (g + 1) * PER):
            if d:
                plane_copy(d).wait_recv()
        each(MATES, lambda d: mate_copy(g, d).start())

    r1_each(lambda c: r1_copy(c).start())
    pass_on(0)

    @pl.when(yc < CHUNKS)
    def _():
        def arrived(d):
            return copy(part.at[0], red1.at[d], r1_s.at[0], r1_r.at[d], mate_peer(1))

        each(MATES, lambda d: arrived(d).wait_recv())
        red1[0] = part[yc]
        total = red1[lax.rem(yc, MATES)]
        for m in range(1, MATES):
            total += red1[lax.rem(yc - m + MATES, MATES)]
        mine[0] = total
        each(PLANES, lambda d: r2_copy(d).start())

    pass_on(1)

    @pl.when(yc < CHUNKS)
    def _():
        each(PLANES, lambda d: r2_copy(d).wait_recv())
        red2[0] = mine[0]
        total = red2[lax.rem(z, PLANES)]
        for m in range(1, PLANES):
            total += red2[lax.rem(z - m + PLANES, PLANES)]
        mine[1] = total
        red3[yc] = total
        each(MATES, lambda d: r3_copy(d).start())

    pass_on(2)
    pass_on(3)

    lane = lax.broadcasted_iota(jnp.int32, (8, 128), 1)
    ids = jnp.zeros((8, 128), jnp.float32)
    for d in range(PLANES):
        ids = jnp.where(lane // 8 == d, planes[d, MATES].astype(jnp.float32), ids)
    names[...] = ids
    each(MATES, lambda d: name_copy(d).start())

    for c in range(CHUNKS):
        @pl.when(yc != c)
        def _():
            copy(mine.at[1], red3.at[c], r3_s.at[0], r3_r.at[c], mate_peer(1)).wait_recv()

    count = red3[4, 1:2, :]
    every = red3[4, 0:1, :] / count
    row = lax.broadcasted_iota(jnp.int32, (NR, 128), 0)
    column = lax.broadcasted_iota(jnp.int32, (NR, 128), 1)
    own = jnp.sum(jnp.where(column == lev * NR + row, every, 0.0), axis=1, keepdims=True)
    gram = jnp.concatenate([red3[c] for c in range(4)], 0)
    cov_ref[...] = gram / count - own * every
    comp = red3[4, 4:8, :] / count
    comp = jnp.concatenate([comp[b : b + 1] for b in range(4)], 1)
    high = comp.astype(jnp.bfloat16).astype(jnp.float32)
    middle = (comp - high).astype(jnp.bfloat16).astype(jnp.float32)
    terms = jnp.concatenate([high, middle, comp - high - middle], 0).astype(jnp.bfloat16)
    terms = jnp.dot(terms, unsort_ref[...], preferred_element_type=jnp.float32)
    comp_ref[...] = terms[0:1] + terms[1:2] + terms[2:3]

    named[0] = names[...]
    mates[0] = planes[:, yc]
    line = lax.broadcasted_iota(jnp.int32, (128, 128), 0)
    lane = lax.broadcasted_iota(jnp.int32, (128, 128), 1)
    wanted = jnp.where(lane % 4 == line // POINTS_DEV, line % POINTS_DEV, -9).astype(jnp.float32)
    each(MATES, lambda d: name_copy(d).wait_recv())
    picked = jnp.zeros((128, 128), jnp.float32)
    for g in range(GROUPS):
        each(MATES, lambda d: mate_copy(g, d).wait_recv())
    for d in range(MATES):
        hit = jnp.where(wanted == named[d, pl.ds(yc, 1), :], 1.0, 0.0).astype(jnp.bfloat16)
        rows = mates[d].astype(jnp.float32).reshape(128, 128).astype(jnp.bfloat16)
        picked += jnp.dot(hit, rows, preferred_element_type=jnp.float32)
    wide = jnp.concatenate([picked[b * POINTS_DEV : (b + 1) * POINTS_DEV] for b in range(4)], 1).astype(jnp.bfloat16)
    out_ref[...] = jnp.dot(wide, unsort_ref[...], preferred_element_type=jnp.float32).astype(jnp.bfloat16)

    each(LEVS, lambda d: prof_copy(d).wait_send())
    each(PLANES, lambda d: plane_copy(d).wait_send())
    each(MATES, lambda d: name_copy(d).wait_send())
    for g in range(GROUPS):
        each(MATES, lambda d: mate_copy(g, d).wait_send())
    r1_each(lambda c: r1_copy(c).wait_send())

    @pl.when(yc < CHUNKS)
    def _():
        each(PLANES, lambda d: r2_copy(d).wait_send())
        each(MATES, lambda d: r3_copy(d).wait_send())


def body(field, patch_list, track_time, track_row, track_col):
    stretch, weights, across, mean, unsort = tables()
    smem = pl.BlockSpec(memory_space=pltpu.SMEM)
    vmem = pl.BlockSpec(memory_space=pltpu.VMEM)
    f32, bf16 = jnp.float32, jnp.bfloat16
    send, prof, sums = pl.pallas_call(
        regrid_kernel,
        out_shape=(
            jax.ShapeDtypeStruct((PLANES, MATES + 1, 8, 128), bf16),
            jax.ShapeDtypeStruct((NR, OWNERS * SLOTS), f32),
            jax.ShapeDtypeStruct((8, 128), f32),
        ),
        in_specs=[smem] * 5 + [vmem] * 4,
        out_specs=(vmem,) * 3,
        scratch_shapes=[pltpu.VMEM((2, 3, SIZE, 128), f32), pltpu.VMEM((OWNERS * 8, 128), f32)],
        compiler_params=pltpu.CompilerParams(vmem_limit_bytes=40 << 20),
        name="regrid",
    )(
        patch_list.reshape(-1), track_time, track_row, track_col, jnp.asarray(stretch),
        field, jnp.asarray(weights), jnp.asarray(across), jnp.asarray(mean),
    )
    dma = pltpu.SemaphoreType.DMA
    out, comp, cov = pl.pallas_call(
        exchange_kernel,
        out_shape=(
            jax.ShapeDtypeStruct((POINTS_DEV, NR * NA), bf16),
            jax.ShapeDtypeStruct((1, NR * NA), f32),
            jax.ShapeDtypeStruct((NR, 128), f32),
        ),
        in_specs=[vmem] * 4,
        out_specs=(vmem,) * 3,
        scratch_shapes=[
            pltpu.VMEM((PLANES, MATES + 1, 8, 128), bf16),
            pltpu.VMEM((MATES, PLANES, 8, 128), bf16),
            pltpu.VMEM((8, 128), f32),
            pltpu.VMEM((MATES, 8, 128), f32),
            pltpu.VMEM((LEVS, NR, OWNERS * SLOTS), f32),
            pltpu.VMEM((CHUNKS, 8, 128), f32),
            pltpu.VMEM((MATES, 8, 128), f32),
            pltpu.VMEM((PLANES, 8, 128), f32),
            pltpu.VMEM((MATES, 8, 128), f32),
            pltpu.VMEM((2, 8, 128), f32),
            dma((PLANES,)), dma((PLANES,)), dma((GROUPS, MATES)), dma((GROUPS, MATES)), dma((MATES,)), dma((MATES,)),
            dma((LEVS,)), dma((LEVS,)), dma((MATES,)), dma((MATES,)), dma((PLANES,)), dma((PLANES,)),
            dma((MATES,)), dma((MATES,)),
        ],
        compiler_params=pltpu.CompilerParams(collective_id=0, has_side_effects=True, vmem_limit_bytes=40 << 20),
        name="exchange",
    )(send, prof, sums, jnp.asarray(unsort))
    return out[:, None, :], comp, cov


def solution(mesh):
    return jax.shard_map(
        body,
        mesh=mesh,
        in_specs=(P("tm", "lev", None, None), P("tm", None, None), P(), P(), P()),
        out_specs=(P("tm", "lev", None), P("lev", None), P("lev", None)),
        check_vma=False,
    )
```

```python
import functools
import math

import jax
import jax.numpy as jnp
import numpy as np
from jax import lax
from jax.experimental import pallas as pl
from jax.experimental.pallas import tpu as pltpu
from jax.sharding import PartitionSpec as P

PATCH, NR, NA = 128, 32, 16
HALF = PATCH // 2
SIZE = 384
POINTS_DEV = 32
OWNERS, SLOTS = 128, 2
PLANES, MATES, LEVS = 16, 8, 4
SPAN = 56
TILES = ((0, 5), (4, 7), (0, 2), (1, 7))
REACH = (48, 1)
GROUPS = 4
CHUNKS = 5
ROUND = 2
HELD = 6


def tables():
    with jax.ensure_compile_time_eval():
        cycle = jnp.arange(NR, dtype=jnp.float32)
        turn = jnp.arange(NA, dtype=jnp.float32)
        radius = (cycle[:, None] + 1.0) * (5.0 * PATCH / (16.0 * NR))
        theta = turn[None, :] * (2.0 * math.pi / NA)
        across = np.asarray((radius * jnp.cos(theta)).reshape(-1))
        along = (radius * jnp.sin(theta)).reshape(-1)
        pos = 0.5 * PATCH + along
        low = jnp.floor(pos)
        frac = pos - low
        upper = np.asarray(frac.astype(jnp.bfloat16)).astype(np.float32)
        lower = np.asarray((1.0 - frac).astype(jnp.bfloat16)).astype(np.float32)
        low = np.asarray(low.astype(jnp.int32))
        latitude = 0.25 * (0.5 * (SIZE - 1) - jnp.arange(SIZE, dtype=jnp.float32))
        stretch = np.asarray(1.0 / jnp.cos(latitude * (math.pi / 180.0)))
    turns = np.arange(NR * NA) % NA
    key = np.where(turns == NA // 4, -1e-3, np.where(turns == 3 * NA // 4, 1e-3, across))
    order = np.argsort(key, kind="stable")
    q = np.arange(NR * NA)
    weights = np.zeros((PATCH, NR * NA), np.float32)
    weights[low[order], q] += lower[order]
    weights[low[order] + 1, q] += upper[order]
    mean = np.zeros((4, NR, 128), np.float32)
    mean[q // 128, order // NA, q % 128] = 1.0 / NA
    unsort = np.zeros((NR * NA, NR * NA), np.float32)
    unsort[q, order] = 1.0
    spread = np.ascontiguousarray(np.broadcast_to(across[order].reshape(4, 1, 128), (4, 8, 128)), np.float32)
    return stretch, weights.astype(jnp.bfloat16), spread, mean, unsort.astype(jnp.bfloat16)


def merge(a, b, step, mask):
    if step == 4:
        return jnp.where(mask, a, b) + pltpu.roll(jnp.where(mask, b, a), 4, 0)
    return jnp.where(mask, a + pltpu.roll(a, 8 - step, 0), b + pltpu.roll(b, step, 0))


def kernel(
    field_hbm, list_hbm, time_hbm, row_hbm, col_hbm, stretch_hbm, weights_hbm, across_hbm, mean_hbm, unsort_hbm,
    out_ref, comp_ref, cov_ref,
    field_ref, list_ref, time_ref, row_ref, col_ref, stretch_ref, weights_ref, across_ref, mean_ref, unsort_ref, load_s,
    turned, polar, send_ref,
    planes, mates, names, named, profs, part, red1, red2, red3, mine,
    plane_s, plane_r, mate_s, mate_r, name_s, name_r, prof_s, prof_r, r1_s, r1_r, r2_s, r2_r, r3_s, r3_r,
):
    tm, lev = lax.axis_index("tm"), lax.axis_index("lev")
    z, yc = tm // MATES, lax.rem(tm, MATES)
    PER = PLANES // GROUPS

    def distance(i):
        half = (i + 1) // 2
        return lax.rem(PLANES // 2 + jnp.where(lax.rem(i, 2) == 1, half, -half), PLANES)

    def plane_peer(d):
        return {"tm": lax.rem(z + d, PLANES) * MATES + yc}

    def mate_peer(d):
        return {"tm": z * MATES + lax.rem(yc + d, MATES)}

    def lev_peer(d):
        return {"lev": lax.rem(lev + d, LEVS)}

    def copy(src, dst, s, r, peer):
        return pltpu.make_async_remote_copy(
            src_ref=src, dst_ref=dst, send_sem=s, recv_sem=r, device_id=peer, device_id_type=pl.DeviceIdType.MESH
        )

    def each(n, f):
        def step(i, c):
            f(i)
            return c

        lax.fori_loop(1, n, step, 0)

    barrier = pltpu.get_barrier_semaphore()

    def greet(peer):
        pl.semaphore_signal(barrier, inc=1, device_id=peer, device_id_type=pl.DeviceIdType.MESH)

    each(PLANES, lambda i: greet(plane_peer(distance(i - 1))))
    loads = [
        pltpu.make_async_copy(src, dst, load_s.at[i])
        for i, (src, dst) in enumerate((
            (field_hbm, field_ref), (list_hbm, list_ref), (time_hbm, time_ref), (row_hbm, row_ref), (col_hbm, col_ref),
            (stretch_hbm, stretch_ref), (weights_hbm, weights_ref), (across_hbm, across_ref), (mean_hbm, mean_ref),
            (unsort_hbm, unsort_ref),
        ))
    ]
    for load in loads:
        load.start()
    each(LEVS, lambda d: greet(lev_peer(d)))
    each(MATES, lambda d: greet(mate_peer(d)))


    def prof_copy(d):
        return copy(profs.at[0], profs.at[d], prof_s.at[d], prof_r.at[d], lev_peer(d))

    def plane_copy(i):
        d = distance(i)
        there = lax.rem(z + d, PLANES)
        return copy(send_ref.at[there], planes.at[i], plane_s.at[i], plane_r.at[i], plane_peer(d))

    def mate_copy(g, d):
        there = lax.rem(yc + d, MATES)
        return copy(
            planes.at[pl.ds(g * PER, PER), there], mates.at[d, pl.ds(g * PER, PER)],
            mate_s.at[g, d], mate_r.at[g, d], mate_peer(d),
        )

    def name_copy(d):
        return copy(names, named.at[d], name_s.at[d], name_r.at[d], mate_peer(d))

    for load in loads[:9]:
        load.wait()
    for t in range(2):
        for i in range(3):
            for j in range(3):
                tile = field_ref[t, 0, i * 128 : (i + 1) * 128, j * 128 : (j + 1) * 128]
                turned[t, i, j * 128 : (j + 1) * 128, :] = tile.astype(jnp.float32).T
    sub = lax.broadcasted_iota(jnp.int32, (8, 128), 0)
    first = (lax.broadcasted_iota(jnp.int32, (8, 128), 1) & 4) == 0
    lane = lax.broadcasted_iota(jnp.int32, (SPAN, 128), 1)
    from_start = [reach - sub.astype(jnp.float32) for reach in REACH]
    m4, m2, m1 = sub < 4, (sub & 2) == 0, (sub & 1) == 0


    def regrid(step, carry):
        total, count = carry
        halves, info = ([], []), []
        planes_now = [lax.rem(z + distance(step * ROUND + r), PLANES) for r in range(ROUND)]
        for g in planes_now:
            points = jnp.zeros((8, 128), jnp.int32)
            for o in range(MATES):
                owner = g * MATES + o
                ids = [list_ref[p, owner] for p in range(SLOTS)]
                for k in ids:
                    point = owner * POINTS_DEV + jnp.maximum(k, 0)
                    t = jnp.clip(time_ref[point] - 2 * tm, 0, 1)
                    row = jnp.clip(row_ref[point], HALF, SIZE - HALF)
                    col = jnp.clip(col_ref[point], HALF, SIZE - HALF)
                    top = row - HALF
                    b = jnp.minimum(top // 128, 1)
                    off = top - b * 128
                    for h in range(2):
                        start = col - REACH[h]
                        one = turned[t, b, pl.ds(start, SPAN), :]
                        two = turned[t, b + 1, pl.ds(start, SPAN), :]
                        halves[h].append(pltpu.roll(jnp.where(lane >= off, one, two), 128 - off, 1))
                    live = jnp.where(k >= 0, 1.0, 0.0)
                    count += live
                    info.append((stretch_ref[row], live))
                points = jnp.where(sub == o, jnp.where(first, ids[0], ids[1]), points)
            send_ref[g, MATES] = points.astype(jnp.float32).astype(jnp.bfloat16)
        mixed = [
            jnp.dot(
                jnp.concatenate(halves[h], 0).astype(jnp.bfloat16),
                weights_ref[:, h * 256 : (h + 1) * 256],
                preferred_element_type=jnp.float32,
            )
            for h in range(2)
        ]
        for o in range(ROUND * MATES):
            g = planes_now[o // MATES]
            accs = []
            for n in (2 * o, 2 * o + 1):
                for blk in range(4):
                    base = across_ref[blk] * info[n][0] + from_start[blk // 2]
                    acc = None
                    for tile in range(*TILES[blk]):
                        w = jnp.maximum(1.0 - jnp.abs(base - 8.0 * tile), 0.0)
                        at = n * SPAN + tile * 8
                        v = mixed[blk // 2][at : at + 8, (blk % 2) * 128 : (blk % 2 + 1) * 128]
                        acc = w * v if acc is None else acc + w * v
                    accs.append(acc)
            a = [accs[i] for i in (0, 4, 2, 6, 1, 5, 3, 7)]
            a = [merge(a[i], a[i + 1], 4, m4) for i in (0, 2, 4, 6)]
            a = [merge(a[i], a[i + 1], 2, m2) for i in (0, 2)]
            out = merge(a[0], a[1], 1, m1) * jnp.where(m4, info[2 * o][1], info[2 * o + 1][1])
            polar[pl.ds(pl.multiple_of((g * MATES + o % MATES) * 8, 8), 8), :] = out
            send_ref[g, o % MATES] = out.astype(jnp.bfloat16)
            total = total + out

        @pl.when(step == HELD // ROUND - 1)
        def _():
            pl.semaphore_wait(barrier, LEVS + MATES + PLANES - 3)
            for j in range(HELD):
                plane_copy(j).start()

        for r in range(ROUND):
            i = step * ROUND + r

            @pl.when(jnp.logical_and(i >= HELD, i < PLANES - 1))
            def _():
                plane_copy(i).start()

        return total, count

    total, count = lax.fori_loop(0, PLANES // ROUND, regrid, (jnp.zeros((8, 128), jnp.float32), 0.0))
    acc = jnp.zeros((NR, OWNERS * SLOTS), jnp.float32)
    for b in range(4):
        acc += lax.dot_general(
            mean_ref[b], polar[pl.ds(b, OWNERS * SLOTS, stride=4), :], (((1,), (1,)), ((), ())),
            precision=lax.Precision.HIGHEST, preferred_element_type=jnp.float32,
        )
    profs[0] = acc
    each(LEVS, lambda d: prof_copy(d).start())
    sums = jnp.where(m4, jnp.where(sub == 1, count, 0.0), total + pltpu.roll(total, 4, 0))
    planes[PLANES - 1] = send_ref[z]

    each(LEVS, lambda d: prof_copy(d).wait_recv())
    whole = jnp.concatenate([profs[lax.rem(lev - l + LEVS, LEVS)] for l in range(LEVS)], 0)
    both = lax.dot_general(
        jnp.concatenate([acc, jnp.ones((8, OWNERS * SLOTS), jnp.float32)], 0), whole, (((1,), (1,)), ((), ())),
        precision=lax.Precision.HIGHEST, preferred_element_type=jnp.float32,
    )
    for c in range(4):
        part[c] = both[c * 8 : (c + 1) * 8]
    part[4] = jnp.where(sub == 0, both[32:40], sums)

    def r1_copy(c):
        d = lax.rem(c - yc + MATES, MATES)
        return copy(part.at[c], red1.at[d], r1_s.at[c], r1_r.at[d], {"tm": z * MATES + c})

    def r2_copy(d):
        return copy(mine.at[0], red2.at[d], r2_s.at[d], r2_r.at[d], plane_peer(d))

    def r3_copy(d):
        return copy(mine.at[1], red3.at[yc], r3_s.at[d], r3_r.at[yc], mate_peer(d))

    def r1_each(f):
        for c in range(CHUNKS):
            @pl.when(yc != c)
            def _():
                f(c)

    def pass_on(g):
        for i in range(g * PER, (g + 1) * PER):
            if i < PLANES - 1:
                plane_copy(i).wait_recv()
        each(MATES, lambda d: mate_copy(g, d).start())

    r1_each(lambda c: r1_copy(c).start())
    pass_on(0)

    @pl.when(yc < CHUNKS)
    def _():
        def arrived(d):
            return copy(part.at[0], red1.at[d], r1_s.at[0], r1_r.at[d], mate_peer(1))

        each(MATES, lambda d: arrived(d).wait_recv())
        red1[0] = part[yc]
        total = red1[lax.rem(yc, MATES)]
        for m in range(1, MATES):
            total += red1[lax.rem(yc - m + MATES, MATES)]
        mine[0] = total
        each(PLANES, lambda i: r2_copy(distance(i - 1)).start())

    pass_on(1)

    @pl.when(yc < CHUNKS)
    def _():
        each(PLANES, lambda d: r2_copy(d).wait_recv())
        red2[0] = mine[0]
        total = red2[lax.rem(z, PLANES)]
        for m in range(1, PLANES):
            total += red2[lax.rem(z - m + PLANES, PLANES)]
        mine[1] = total
        red3[yc] = total
        each(MATES, lambda d: r3_copy(d).start())

    pass_on(2)
    pass_on(3)

    lane = lax.broadcasted_iota(jnp.int32, (8, 128), 1)
    ids = jnp.zeros((8, 128), jnp.float32)
    for d in range(PLANES):
        ids = jnp.where(lane // 8 == d, planes[d, MATES].astype(jnp.float32), ids)
    names[...] = ids
    each(MATES, lambda d: name_copy(d).start())

    for c in range(CHUNKS):
        @pl.when(yc != c)
        def _():
            copy(mine.at[1], red3.at[c], r3_s.at[0], r3_r.at[c], mate_peer(1)).wait_recv()

    loads[9].wait()
    count = red3[4, 1:2, :]
    every = red3[4, 0:1, :] / count
    row = lax.broadcasted_iota(jnp.int32, (NR, 128), 0)
    column = lax.broadcasted_iota(jnp.int32, (NR, 128), 1)
    own = jnp.sum(jnp.where(column == lev * NR + row, every, 0.0), axis=1, keepdims=True)
    gram = jnp.concatenate([red3[c] for c in range(4)], 0)
    cov_ref[...] = gram / count - own * every
    comp = red3[4, 4:8, :] / count
    comp = jnp.concatenate([comp[b : b + 1] for b in range(4)], 1)
    high = comp.astype(jnp.bfloat16).astype(jnp.float32)
    middle = (comp - high).astype(jnp.bfloat16).astype(jnp.float32)
    terms = jnp.concatenate([high, middle, comp - high - middle], 0).astype(jnp.bfloat16)
    terms = jnp.dot(terms, unsort_ref[...], preferred_element_type=jnp.float32)
    comp_ref[...] = terms[0:1] + terms[1:2] + terms[2:3]

    named[0] = names[...]
    mates[0] = planes[:, yc]
    line = lax.broadcasted_iota(jnp.int32, (128, 128), 0)
    lane = lax.broadcasted_iota(jnp.int32, (128, 128), 1)
    wanted = jnp.where(lane % 4 == line // POINTS_DEV, line % POINTS_DEV, -9).astype(jnp.float32)
    each(MATES, lambda d: name_copy(d).wait_recv())
    picked = jnp.zeros((128, 128), jnp.float32)
    for g in range(GROUPS):
        each(MATES, lambda d: mate_copy(g, d).wait_recv())
    for d in range(MATES):
        hit = jnp.where(wanted == named[d, pl.ds(yc, 1), :], 1.0, 0.0).astype(jnp.bfloat16)
        rows = mates[d].astype(jnp.float32).reshape(128, 128).astype(jnp.bfloat16)
        picked += jnp.dot(hit, rows, preferred_element_type=jnp.float32)
    wide = jnp.concatenate([picked[b * POINTS_DEV : (b + 1) * POINTS_DEV] for b in range(4)], 1).astype(jnp.bfloat16)
    out_ref[...] = jnp.dot(wide, unsort_ref[...], preferred_element_type=jnp.float32).astype(jnp.bfloat16)

    each(LEVS, lambda d: prof_copy(d).wait_send())
    each(PLANES, lambda i: plane_copy(i - 1).wait_send())
    each(MATES, lambda d: name_copy(d).wait_send())
    for g in range(GROUPS):
        each(MATES, lambda d: mate_copy(g, d).wait_send())
    r1_each(lambda c: r1_copy(c).wait_send())

    @pl.when(yc < CHUNKS)
    def _():
        each(PLANES, lambda d: r2_copy(d).wait_send())
        each(MATES, lambda d: r3_copy(d).wait_send())


def body(field, patch_list, track_time, track_row, track_col):
    stretch, weights, across, mean, unsort = tables()
    smem, vmem, dma = pltpu.SMEM, pltpu.VMEM, pltpu.SemaphoreType.DMA
    i32, f32, bf16 = jnp.int32, jnp.float32, jnp.bfloat16
    out, comp, cov = pl.pallas_call(
        kernel,
        out_shape=(
            jax.ShapeDtypeStruct((POINTS_DEV, NR * NA), bf16),
            jax.ShapeDtypeStruct((1, NR * NA), f32),
            jax.ShapeDtypeStruct((NR, 128), f32),
        ),
        in_specs=[pl.BlockSpec(memory_space=pl.ANY)] * 10,
        out_specs=(pl.BlockSpec(memory_space=vmem),) * 3,
        scratch_shapes=[
            vmem(field.shape, bf16), smem((SLOTS, OWNERS), i32),
            smem(track_time.shape, i32), smem(track_row.shape, i32), smem(track_col.shape, i32),
            smem(stretch.shape, f32), vmem(weights.shape, bf16), vmem(across.shape, f32), vmem(mean.shape, f32),
            vmem(unsort.shape, bf16), dma((10,)),
            vmem((2, 3, SIZE, 128), f32), vmem((OWNERS * 8, 128), f32), vmem((PLANES, MATES + 1, 8, 128), bf16),
            vmem((PLANES, MATES + 1, 8, 128), bf16), vmem((MATES, PLANES, 8, 128), bf16),
            vmem((8, 128), f32), vmem((MATES, 8, 128), f32), vmem((LEVS, NR, OWNERS * SLOTS), f32),
            vmem((CHUNKS, 8, 128), f32), vmem((MATES, 8, 128), f32), vmem((PLANES, 8, 128), f32),
            vmem((MATES, 8, 128), f32), vmem((2, 8, 128), f32),
            dma((PLANES,)), dma((PLANES,)), dma((GROUPS, MATES)), dma((GROUPS, MATES)), dma((MATES,)), dma((MATES,)),
            dma((LEVS,)), dma((LEVS,)), dma((MATES,)), dma((MATES,)), dma((PLANES,)), dma((PLANES,)),
            dma((MATES,)), dma((MATES,)),
        ],
        compiler_params=pltpu.CompilerParams(collective_id=0, has_side_effects=True, vmem_limit_bytes=60 << 20),
        name="composites",
    )(
        field, patch_list[0].T, track_time, track_row, track_col,
        jnp.asarray(stretch), jnp.asarray(weights), jnp.asarray(across), jnp.asarray(mean), jnp.asarray(unsort),
    )
    return out[:, None, :], comp, cov


def solution(mesh):
    return jax.shard_map(
        body,
        mesh=mesh,
        in_specs=(P("tm", "lev", None, None), P("tm", None, None), P(), P(), P()),
        out_specs=(P("tm", "lev", None), P("lev", None), P("lev", None)),
        check_vma=False,
    )
```

```python
import functools
import math

import jax
import jax.numpy as jnp
import numpy as np
from jax import lax
from jax.experimental import pallas as pl
from jax.experimental.pallas import tpu as pltpu
from jax.sharding import PartitionSpec as P

PATCH, NR, NA = 128, 32, 16
HALF = PATCH // 2
SIZE = 384
POINTS_DEV = 32
OWNERS, SLOTS = 128, 2
PLANES, MATES, LEVS = 16, 8, 4
SPAN = 56
TILES = ((0, 5), (4, 7), (0, 2), (1, 7))
REACH = (48, 1)
GROUPS = 4
CHUNKS = 5
ROUND = 2
HELD = 8


def tables():
    with jax.ensure_compile_time_eval():
        cycle = jnp.arange(NR, dtype=jnp.float32)
        turn = jnp.arange(NA, dtype=jnp.float32)
        radius = (cycle[:, None] + 1.0) * (5.0 * PATCH / (16.0 * NR))
        theta = turn[None, :] * (2.0 * math.pi / NA)
        across = np.asarray((radius * jnp.cos(theta)).reshape(-1))
        along = (radius * jnp.sin(theta)).reshape(-1)
        pos = 0.5 * PATCH + along
        low = jnp.floor(pos)
        frac = pos - low
        upper = np.asarray(frac.astype(jnp.bfloat16)).astype(np.float32)
        lower = np.asarray((1.0 - frac).astype(jnp.bfloat16)).astype(np.float32)
        low = np.asarray(low.astype(jnp.int32))
        latitude = 0.25 * (0.5 * (SIZE - 1) - jnp.arange(SIZE, dtype=jnp.float32))
        stretch = np.asarray(1.0 / jnp.cos(latitude * (math.pi / 180.0)))
    turns = np.arange(NR * NA) % NA
    key = np.where(turns == NA // 4, -1e-3, np.where(turns == 3 * NA // 4, 1e-3, across))
    order = np.argsort(key, kind="stable")
    q = np.arange(NR * NA)
    weights = np.zeros((PATCH, NR * NA), np.float32)
    weights[low[order], q] += lower[order]
    weights[low[order] + 1, q] += upper[order]
    mean = np.zeros((NR, 4, 3, 128), np.float32)
    mean[order // NA, q // 128, :, q % 128] = 1.0 / NA
    mean = mean.reshape(NR, -1).astype(jnp.bfloat16)
    unsort = np.zeros((NR * NA, NR * NA), np.float32)
    unsort[q, order] = 1.0
    spread = np.ascontiguousarray(np.broadcast_to(across[order].reshape(4, 1, 128), (4, 8, 128)), np.float32)
    return stretch, weights.astype(jnp.bfloat16), spread, mean, unsort.astype(jnp.bfloat16)


def merge(a, b, step, mask):
    if step == 4:
        return jnp.where(mask, a, b) + pltpu.roll(jnp.where(mask, b, a), 4, 0)
    return jnp.where(mask, a + pltpu.roll(a, 8 - step, 0), b + pltpu.roll(b, step, 0))


def kernel(
    field_hbm, list_hbm, time_hbm, row_hbm, col_hbm, stretch_hbm, weights_hbm, across_hbm, mean_hbm, unsort_hbm,
    out_ref, comp_ref, cov_ref,
    field_ref, list_ref, time_ref, row_ref, col_ref, stretch_ref, weights_ref, across_ref, mean_ref, unsort_ref, load_s,
    turned, polar, send_ref,
    planes, mates, names, named, profs, part, red1, red2, red3, mine,
    plane_s, plane_r, mate_s, mate_r, name_s, name_r, prof_s, prof_r, r1_s, r1_r, r2_s, r2_r, r3_s, r3_r,
):
    tm, lev = lax.axis_index("tm"), lax.axis_index("lev")
    z, yc = tm // MATES, lax.rem(tm, MATES)
    PER = PLANES // GROUPS

    def distance(i):
        half = (i + 1) // 2
        return lax.rem(PLANES // 2 + jnp.where(lax.rem(i, 2) == 1, half, -half), PLANES)

    def plane_peer(d):
        return {"tm": lax.rem(z + d, PLANES) * MATES + yc}

    def mate_peer(d):
        return {"tm": z * MATES + lax.rem(yc + d, MATES)}

    def lev_peer(d):
        return {"lev": lax.rem(lev + d, LEVS)}

    def copy(src, dst, s, r, peer):
        return pltpu.make_async_remote_copy(
            src_ref=src, dst_ref=dst, send_sem=s, recv_sem=r, device_id=peer, device_id_type=pl.DeviceIdType.MESH
        )

    def each(n, f):
        def step(i, c):
            f(i)
            return c

        lax.fori_loop(1, n, step, 0)

    barrier = pltpu.get_barrier_semaphore()

    def greet(peer):
        pl.semaphore_signal(barrier, inc=1, device_id=peer, device_id_type=pl.DeviceIdType.MESH)

    each(PLANES, lambda i: greet(plane_peer(distance(i - 1))))
    loads = [
        pltpu.make_async_copy(src, dst, load_s.at[i])
        for i, (src, dst) in enumerate((
            (field_hbm, field_ref), (list_hbm, list_ref), (time_hbm, time_ref), (row_hbm, row_ref), (col_hbm, col_ref),
            (stretch_hbm, stretch_ref), (weights_hbm, weights_ref), (across_hbm, across_ref), (mean_hbm, mean_ref),
            (unsort_hbm, unsort_ref),
        ))
    ]
    for load in loads:
        load.start()
    each(LEVS, lambda d: greet(lev_peer(d)))
    each(MATES, lambda d: greet(mate_peer(d)))


    def prof_copy(d):
        return copy(profs.at[0], profs.at[d], prof_s.at[d], prof_r.at[d], lev_peer(d))

    def plane_copy(i):
        d = distance(i)
        there = lax.rem(z + d, PLANES)
        return copy(send_ref.at[there], planes.at[i], plane_s.at[i], plane_r.at[i], plane_peer(d))

    def mate_copy(g, d):
        there = lax.rem(yc + d, MATES)
        return copy(
            planes.at[pl.ds(g * PER, PER), there], mates.at[d, pl.ds(g * PER, PER)],
            mate_s.at[g, d], mate_r.at[g, d], mate_peer(d),
        )

    def name_copy(d):
        return copy(names, named.at[d], name_s.at[d], name_r.at[d], mate_peer(d))

    for load in loads[:9]:
        load.wait()
    for t in range(2):
        for i in range(3):
            for j in range(3):
                tile = field_ref[t, 0, i * 128 : (i + 1) * 128, j * 128 : (j + 1) * 128]
                turned[t, i, j * 128 : (j + 1) * 128, :] = tile.astype(jnp.float32).T
    sub = lax.broadcasted_iota(jnp.int32, (8, 128), 0)
    first = (lax.broadcasted_iota(jnp.int32, (8, 128), 1) & 4) == 0
    lane = lax.broadcasted_iota(jnp.int32, (SPAN, 128), 1)
    from_start = [reach - sub.astype(jnp.float32) for reach in REACH]
    m4, m2, m1 = sub < 4, (sub & 2) == 0, (sub & 1) == 0


    def regrid(step, carry):
        total, count = carry
        halves, info = ([], []), []
        planes_now = [lax.rem(z + distance(step * ROUND + r), PLANES) for r in range(ROUND)]
        for g in planes_now:
            points = jnp.zeros((8, 128), jnp.int32)
            for o in range(MATES):
                owner = g * MATES + o
                ids = [list_ref[p, owner] for p in range(SLOTS)]
                for k in ids:
                    point = owner * POINTS_DEV + jnp.maximum(k, 0)
                    t = jnp.clip(time_ref[point] - 2 * tm, 0, 1)
                    row = jnp.clip(row_ref[point], HALF, SIZE - HALF)
                    col = jnp.clip(col_ref[point], HALF, SIZE - HALF)
                    top = row - HALF
                    b = jnp.minimum(top // 128, 1)
                    off = top - b * 128
                    for h in range(2):
                        start = col - REACH[h]
                        one = turned[t, b, pl.ds(start, SPAN), :]
                        two = turned[t, b + 1, pl.ds(start, SPAN), :]
                        halves[h].append(pltpu.roll(jnp.where(lane >= off, one, two), 128 - off, 1))
                    live = jnp.where(k >= 0, 1.0, 0.0)
                    count += live
                    info.append((stretch_ref[row], live))
                points = jnp.where(sub == o, jnp.where(first, ids[0], ids[1]), points)
            send_ref[g, MATES] = points.astype(jnp.float32).astype(jnp.bfloat16)
        mixed = [
            jnp.dot(
                jnp.concatenate(halves[h], 0).astype(jnp.bfloat16),
                weights_ref[:, h * 256 : (h + 1) * 256],
                preferred_element_type=jnp.float32,
            )
            for h in range(2)
        ]
        for o in range(ROUND * MATES):
            g = planes_now[o // MATES]
            accs = []
            for n in (2 * o, 2 * o + 1):
                for blk in range(4):
                    base = across_ref[blk] * info[n][0] + from_start[blk // 2]
                    acc = None
                    for tile in range(*TILES[blk]):
                        w = jnp.maximum(1.0 - jnp.abs(base - 8.0 * tile), 0.0)
                        at = n * SPAN + tile * 8
                        v = mixed[blk // 2][at : at + 8, (blk % 2) * 128 : (blk % 2 + 1) * 128]
                        acc = w * v if acc is None else acc + w * v
                    accs.append(acc)
            a = [accs[i] for i in (0, 4, 2, 6, 1, 5, 3, 7)]
            a = [merge(a[i], a[i + 1], 4, m4) for i in (0, 2, 4, 6)]
            a = [merge(a[i], a[i + 1], 2, m2) for i in (0, 2)]
            out = merge(a[0], a[1], 1, m1) * jnp.where(m4, info[2 * o][1], info[2 * o + 1][1])
            polar[pl.ds(pl.multiple_of((g * MATES + o % MATES) * 8, 8), 8), :] = out
            send_ref[g, o % MATES] = out.astype(jnp.bfloat16)
            total = total + out

        @pl.when(step == HELD // ROUND - 1)
        def _():
            pl.semaphore_wait(barrier, LEVS + MATES + PLANES - 3)
            for j in range(HELD):
                plane_copy(j).start()

        for r in range(ROUND):
            i = step * ROUND + r

            @pl.when(jnp.logical_and(i >= HELD, i < PLANES - 1))
            def _():
                plane_copy(i).start()

        return total, count

    total, count = lax.fori_loop(0, PLANES // ROUND, regrid, (jnp.zeros((8, 128), jnp.float32), 0.0))
    parts = []
    for b in range(4):
        value = polar[pl.ds(b, OWNERS * SLOTS, stride=4), :]
        for _ in range(3):
            term = value.astype(jnp.bfloat16)
            parts.append(term)
            value = value - term.astype(jnp.float32)
    acc = lax.dot_general(
        mean_ref[...], jnp.concatenate(parts, 1), (((1,), (1,)), ((), ())), preferred_element_type=jnp.float32
    )
    profs[0] = acc
    each(LEVS, lambda d: prof_copy(d).start())
    sums = jnp.where(m4, jnp.where(sub == 1, count, 0.0), total + pltpu.roll(total, 4, 0))
    planes[PLANES - 1] = send_ref[z]

    each(LEVS, lambda d: prof_copy(d).wait_recv())
    whole = jnp.concatenate([profs[lax.rem(lev - l + LEVS, LEVS)] for l in range(LEVS)], 0)
    both = lax.dot_general(
        jnp.concatenate([acc, jnp.ones((8, OWNERS * SLOTS), jnp.float32)], 0), whole, (((1,), (1,)), ((), ())),
        precision=lax.Precision.HIGHEST, preferred_element_type=jnp.float32,
    )
    for c in range(4):
        part[c] = both[c * 8 : (c + 1) * 8]
    part[4] = jnp.where(sub == 0, both[32:40], sums)

    def r1_copy(c):
        d = lax.rem(c - yc + MATES, MATES)
        return copy(part.at[c], red1.at[d], r1_s.at[c], r1_r.at[d], {"tm": z * MATES + c})

    def r2_copy(d):
        return copy(mine.at[0], red2.at[d], r2_s.at[d], r2_r.at[d], plane_peer(d))

    def r3_copy(d):
        return copy(mine.at[1], red3.at[yc], r3_s.at[d], r3_r.at[yc], mate_peer(d))

    def r1_each(f):
        for c in range(CHUNKS):
            @pl.when(yc != c)
            def _():
                f(c)

    def pass_on(g):
        for i in range(g * PER, (g + 1) * PER):
            if i < PLANES - 1:
                plane_copy(i).wait_recv()
        each(MATES, lambda d: mate_copy(g, d).start())

    r1_each(lambda c: r1_copy(c).start())

    @pl.when(yc < CHUNKS)
    def _():
        def arrived(d):
            return copy(part.at[0], red1.at[d], r1_s.at[0], r1_r.at[d], mate_peer(1))

        each(MATES, lambda d: arrived(d).wait_recv())
        red1[0] = part[yc]
        total = red1[lax.rem(yc, MATES)]
        for m in range(1, MATES):
            total += red1[lax.rem(yc - m + MATES, MATES)]
        mine[0] = total
        each(PLANES, lambda i: r2_copy(distance(i - 1)).start())

    pass_on(0)
    pass_on(1)

    @pl.when(yc < CHUNKS)
    def _():
        each(PLANES, lambda d: r2_copy(d).wait_recv())
        red2[0] = mine[0]
        total = red2[lax.rem(z, PLANES)]
        for m in range(1, PLANES):
            total += red2[lax.rem(z - m + PLANES, PLANES)]
        mine[1] = total
        red3[yc] = total
        each(MATES, lambda d: r3_copy(d).start())

    pass_on(2)
    pass_on(3)

    lane = lax.broadcasted_iota(jnp.int32, (8, 128), 1)
    ids = jnp.zeros((8, 128), jnp.float32)
    for d in range(PLANES):
        ids = jnp.where(lane // 8 == d, planes[d, MATES].astype(jnp.float32), ids)
    names[...] = ids
    each(MATES, lambda d: name_copy(d).start())

    for c in range(CHUNKS):
        @pl.when(yc != c)
        def _():
            copy(mine.at[1], red3.at[c], r3_s.at[0], r3_r.at[c], mate_peer(1)).wait_recv()

    loads[9].wait()
    count = red3[4, 1:2, :]
    every = red3[4, 0:1, :] / count
    row = lax.broadcasted_iota(jnp.int32, (NR, 128), 0)
    column = lax.broadcasted_iota(jnp.int32, (NR, 128), 1)
    own = jnp.sum(jnp.where(column == lev * NR + row, every, 0.0), axis=1, keepdims=True)
    gram = jnp.concatenate([red3[c] for c in range(4)], 0)
    cov_ref[...] = gram / count - own * every
    comp = red3[4, 4:8, :] / count
    comp = jnp.concatenate([comp[b : b + 1] for b in range(4)], 1)
    high = comp.astype(jnp.bfloat16).astype(jnp.float32)
    middle = (comp - high).astype(jnp.bfloat16).astype(jnp.float32)
    terms = jnp.concatenate([high, middle, comp - high - middle], 0).astype(jnp.bfloat16)
    terms = jnp.dot(terms, unsort_ref[...], preferred_element_type=jnp.float32)
    comp_ref[...] = terms[0:1] + terms[1:2] + terms[2:3]

    named[0] = names[...]
    mates[0] = planes[:, yc]
    line = lax.broadcasted_iota(jnp.int32, (128, 128), 0)
    lane = lax.broadcasted_iota(jnp.int32, (128, 128), 1)
    wanted = jnp.where(lane % 4 == line // POINTS_DEV, line % POINTS_DEV, -9).astype(jnp.float32)
    each(MATES, lambda d: name_copy(d).wait_recv())
    picked = jnp.zeros((128, 128), jnp.float32)
    for g in range(GROUPS):
        each(MATES, lambda d: mate_copy(g, d).wait_recv())
    for d in range(MATES):
        hit = jnp.where(wanted == named[d, pl.ds(yc, 1), :], 1.0, 0.0).astype(jnp.bfloat16)
        rows = mates[d].astype(jnp.float32).reshape(128, 128).astype(jnp.bfloat16)
        picked += jnp.dot(hit, rows, preferred_element_type=jnp.float32)
    wide = jnp.concatenate([picked[b * POINTS_DEV : (b + 1) * POINTS_DEV] for b in range(4)], 1).astype(jnp.bfloat16)
    out_ref[...] = jnp.dot(wide, unsort_ref[...], preferred_element_type=jnp.float32).astype(jnp.bfloat16)

    each(LEVS, lambda d: prof_copy(d).wait_send())
    each(PLANES, lambda i: plane_copy(i - 1).wait_send())
    each(MATES, lambda d: name_copy(d).wait_send())
    for g in range(GROUPS):
        each(MATES, lambda d: mate_copy(g, d).wait_send())
    r1_each(lambda c: r1_copy(c).wait_send())

    @pl.when(yc < CHUNKS)
    def _():
        each(PLANES, lambda d: r2_copy(d).wait_send())
        each(MATES, lambda d: r3_copy(d).wait_send())


def finish_kernel(out_in, comp_in, cov_in, out_ref, comp_ref, cov_ref):
    out_ref[...] = out_in[...]
    comp_ref[...] = comp_in[...]
    cov_ref[...] = cov_in[...]


def body(field, patch_list, track_time, track_row, track_col):
    stretch, weights, across, mean, unsort = tables()
    smem, vmem, dma = pltpu.SMEM, pltpu.VMEM, pltpu.SemaphoreType.DMA
    i32, f32, bf16 = jnp.int32, jnp.float32, jnp.bfloat16
    out, comp, cov = pl.pallas_call(
        kernel,
        out_shape=(
            jax.ShapeDtypeStruct((POINTS_DEV, NR * NA), bf16),
            jax.ShapeDtypeStruct((1, NR * NA), f32),
            jax.ShapeDtypeStruct((NR, 128), f32),
        ),
        in_specs=[pl.BlockSpec(memory_space=pl.ANY)] * 10,
        out_specs=(pl.BlockSpec(memory_space=vmem),) * 3,
        scratch_shapes=[
            vmem(field.shape, bf16), smem((SLOTS, OWNERS), i32),
            smem(track_time.shape, i32), smem(track_row.shape, i32), smem(track_col.shape, i32),
            smem(stretch.shape, f32), vmem(weights.shape, bf16), vmem(across.shape, f32), vmem(mean.shape, bf16),
            vmem(unsort.shape, bf16), dma((10,)),
            vmem((2, 3, SIZE, 128), f32), vmem((OWNERS * 8, 128), f32), vmem((PLANES, MATES + 1, 8, 128), bf16),
            vmem((PLANES, MATES + 1, 8, 128), bf16), vmem((MATES, PLANES, 8, 128), bf16),
            vmem((8, 128), f32), vmem((MATES, 8, 128), f32), vmem((LEVS, NR, OWNERS * SLOTS), f32),
            vmem((CHUNKS, 8, 128), f32), vmem((MATES, 8, 128), f32), vmem((PLANES, 8, 128), f32),
            vmem((MATES, 8, 128), f32), vmem((2, 8, 128), f32),
            dma((PLANES,)), dma((PLANES,)), dma((GROUPS, MATES)), dma((GROUPS, MATES)), dma((MATES,)), dma((MATES,)),
            dma((LEVS,)), dma((LEVS,)), dma((MATES,)), dma((MATES,)), dma((PLANES,)), dma((PLANES,)),
            dma((MATES,)), dma((MATES,)),
        ],
        compiler_params=pltpu.CompilerParams(collective_id=0, has_side_effects=True, vmem_limit_bytes=60 << 20),
        name="composites",
    )(
        field, patch_list[0].T, track_time, track_row, track_col,
        jnp.asarray(stretch), jnp.asarray(weights), jnp.asarray(across), jnp.asarray(mean), jnp.asarray(unsort),
    )
    out, comp, cov = pl.pallas_call(
        finish_kernel,
        out_shape=tuple(jax.ShapeDtypeStruct(a.shape, a.dtype) for a in (out, comp, cov)),
        in_specs=[pl.BlockSpec(memory_space=vmem)] * 3,
        out_specs=(pl.BlockSpec(memory_space=vmem),) * 3,
        name="finish",
    )(out, comp, cov)
    return out[:, None, :], comp, cov


def solution(mesh):
    return jax.shard_map(
        body,
        mesh=mesh,
        in_specs=(P("tm", "lev", None, None), P("tm", None, None), P(), P(), P()),
        out_specs=(P("tm", "lev", None), P("lev", None), P("lev", None)),
        check_vma=False,
    )
```

```python
import functools
import math

import jax
import jax.numpy as jnp
import numpy as np
from jax import lax
from jax.experimental import pallas as pl
from jax.experimental.pallas import tpu as pltpu
from jax.sharding import PartitionSpec as P

PATCH, NR, NA = 128, 32, 16
HALF = PATCH // 2
SIZE = 384
POINTS_DEV = 32
OWNERS, SLOTS = 128, 2
PLANES, MATES, LEVS = 16, 8, 4
SPAN = 56
TILES = ((0, 5), (4, 7), (0, 2), (1, 7))
REACH = (48, 1)
GROUPS = 4
CHUNKS = 5
ROUND = 2
HELD = 8


def tables():
    with jax.ensure_compile_time_eval():
        cycle = jnp.arange(NR, dtype=jnp.float32)
        turn = jnp.arange(NA, dtype=jnp.float32)
        radius = (cycle[:, None] + 1.0) * (5.0 * PATCH / (16.0 * NR))
        theta = turn[None, :] * (2.0 * math.pi / NA)
        across = np.asarray((radius * jnp.cos(theta)).reshape(-1))
        along = (radius * jnp.sin(theta)).reshape(-1)
        pos = 0.5 * PATCH + along
        low = jnp.floor(pos)
        frac = pos - low
        upper = np.asarray(frac.astype(jnp.bfloat16)).astype(np.float32)
        lower = np.asarray((1.0 - frac).astype(jnp.bfloat16)).astype(np.float32)
        low = np.asarray(low.astype(jnp.int32))
        latitude = 0.25 * (0.5 * (SIZE - 1) - jnp.arange(SIZE, dtype=jnp.float32))
        stretch = np.asarray(1.0 / jnp.cos(latitude * (math.pi / 180.0)))
    turns = np.arange(NR * NA) % NA
    key = np.where(turns == NA // 4, -1e-3, np.where(turns == 3 * NA // 4, 1e-3, across))
    order = np.argsort(key, kind="stable")
    q = np.arange(NR * NA)
    weights = np.zeros((PATCH, NR * NA), np.float32)
    weights[low[order], q] += lower[order]
    weights[low[order] + 1, q] += upper[order]
    mean = np.zeros((NR, 4, 3, 128), np.float32)
    mean[order // NA, q // 128, :, q % 128] = 1.0 / NA
    mean = mean.reshape(NR, -1).astype(jnp.bfloat16)
    unsort = np.zeros((NR * NA, NR * NA), np.float32)
    unsort[q, order] = 1.0
    spread = np.ascontiguousarray(np.broadcast_to(across[order].reshape(4, 1, 128), (4, 8, 128)), np.float32)
    return stretch, weights.astype(jnp.bfloat16), spread, mean, unsort.astype(jnp.bfloat16)


def merge(a, b, step, mask):
    if step == 4:
        return jnp.where(mask, a, b) + pltpu.roll(jnp.where(mask, b, a), 4, 0)
    return jnp.where(mask, a + pltpu.roll(a, 8 - step, 0), b + pltpu.roll(b, step, 0))


def kernel(
    field_hbm, list_hbm, time_hbm, row_hbm, col_hbm, stretch_hbm, weights_hbm, across_hbm, mean_hbm, unsort_hbm,
    out_ref, comp_ref, cov_ref,
    field_ref, list_ref, time_ref, row_ref, col_ref, stretch_ref, weights_ref, across_ref, mean_ref, unsort_ref, load_s,
    turned, polar, send_ref,
    planes, mates, names, named, profs, part, red1, red2, red3, mine,
    plane_s, plane_r, mate_s, mate_r, name_s, name_r, prof_s, prof_r, r1_s, r1_r, r2_s, r2_r, r3_s, r3_r,
):
    tm, lev = lax.axis_index("tm"), lax.axis_index("lev")
    z, yc = tm // MATES, lax.rem(tm, MATES)
    PER = PLANES // GROUPS

    def distance(i):
        half = (i + 1) // 2
        return lax.rem(PLANES // 2 + jnp.where(lax.rem(i, 2) == 1, half, -half), PLANES)

    def plane_peer(d):
        return {"tm": lax.rem(z + d, PLANES) * MATES + yc}

    def mate_peer(d):
        return {"tm": z * MATES + lax.rem(yc + d, MATES)}

    def lev_peer(d):
        return {"lev": lax.rem(lev + d, LEVS)}

    def copy(src, dst, s, r, peer):
        return pltpu.make_async_remote_copy(
            src_ref=src, dst_ref=dst, send_sem=s, recv_sem=r, device_id=peer, device_id_type=pl.DeviceIdType.MESH
        )

    def each(n, f):
        def step(i, c):
            f(i)
            return c

        lax.fori_loop(1, n, step, 0)

    barrier = pltpu.get_barrier_semaphore()

    def greet(peer):
        pl.semaphore_signal(barrier, inc=1, device_id=peer, device_id_type=pl.DeviceIdType.MESH)

    loads = [
        pltpu.make_async_copy(src, dst, load_s.at[i])
        for i, (src, dst) in enumerate((
            (field_hbm, field_ref), (list_hbm, list_ref), (time_hbm, time_ref), (row_hbm, row_ref), (col_hbm, col_ref),
            (stretch_hbm, stretch_ref), (weights_hbm, weights_ref), (across_hbm, across_ref), (mean_hbm, mean_ref),
            (unsort_hbm, unsort_ref),
        ))
    ]
    for load in loads:
        load.start()
    each(PLANES, lambda i: greet(plane_peer(distance(i - 1))))
    each(LEVS, lambda d: greet(lev_peer(d)))
    each(MATES, lambda d: greet(mate_peer(d)))


    def prof_copy(d):
        return copy(profs.at[0], profs.at[d], prof_s.at[d], prof_r.at[d], lev_peer(d))

    def plane_copy(i):
        d = distance(i)
        there = lax.rem(z + d, PLANES)
        return copy(send_ref.at[there], planes.at[i], plane_s.at[i], plane_r.at[i], plane_peer(d))

    def mate_copy(g, d):
        there = lax.rem(yc + d, MATES)
        return copy(
            planes.at[pl.ds(g * PER, PER), there], mates.at[d, pl.ds(g * PER, PER)],
            mate_s.at[g, d], mate_r.at[g, d], mate_peer(d),
        )

    def name_copy(d):
        return copy(names, named.at[d], name_s.at[d], name_r.at[d], mate_peer(d))

    loads[0].wait()
    for t in range(2):
        for i in range(3):
            for j in range(3):
                tile = field_ref[t, 0, i * 128 : (i + 1) * 128, j * 128 : (j + 1) * 128]
                turned[t, i, j * 128 : (j + 1) * 128, :] = tile.astype(jnp.float32).T
    for load in loads[1:9]:
        load.wait()
    sub = lax.broadcasted_iota(jnp.int32, (8, 128), 0)
    first = (lax.broadcasted_iota(jnp.int32, (8, 128), 1) & 4) == 0
    lane = lax.broadcasted_iota(jnp.int32, (SPAN, 128), 1)
    from_start = [reach - sub.astype(jnp.float32) for reach in REACH]
    m4, m2, m1 = sub < 4, (sub & 2) == 0, (sub & 1) == 0


    def regrid(step, carry):
        total, count = carry
        halves, info = ([], []), []
        planes_now = [lax.rem(z + distance(step * ROUND + r), PLANES) for r in range(ROUND)]
        for g in planes_now:
            points = jnp.zeros((8, 128), jnp.int32)
            for o in range(MATES):
                owner = g * MATES + o
                ids = [list_ref[p, owner] for p in range(SLOTS)]
                for k in ids:
                    point = owner * POINTS_DEV + jnp.maximum(k, 0)
                    t = jnp.clip(time_ref[point] - 2 * tm, 0, 1)
                    row = jnp.clip(row_ref[point], HALF, SIZE - HALF)
                    col = jnp.clip(col_ref[point], HALF, SIZE - HALF)
                    top = row - HALF
                    b = jnp.minimum(top // 128, 1)
                    off = top - b * 128
                    for h in range(2):
                        start = col - REACH[h]
                        one = turned[t, b, pl.ds(start, SPAN), :]
                        two = turned[t, b + 1, pl.ds(start, SPAN), :]
                        halves[h].append(pltpu.roll(jnp.where(lane >= off, one, two), 128 - off, 1))
                    live = jnp.where(k >= 0, 1.0, 0.0)
                    count += live
                    info.append((stretch_ref[row], live))
                points = jnp.where(sub == o, jnp.where(first, ids[0], ids[1]), points)
            send_ref[g, MATES] = points.astype(jnp.float32).astype(jnp.bfloat16)
        mixed = [
            jnp.dot(
                jnp.concatenate(halves[h], 0).astype(jnp.bfloat16),
                weights_ref[:, h * 256 : (h + 1) * 256],
                preferred_element_type=jnp.float32,
            )
            for h in range(2)
        ]
        for o in range(ROUND * MATES):
            g = planes_now[o // MATES]
            accs = []
            for n in (2 * o, 2 * o + 1):
                for blk in range(4):
                    base = across_ref[blk] * info[n][0] + from_start[blk // 2]
                    acc = None
                    for tile in range(*TILES[blk]):
                        w = jnp.maximum(1.0 - jnp.abs(base - 8.0 * tile), 0.0)
                        at = n * SPAN + tile * 8
                        v = mixed[blk // 2][at : at + 8, (blk % 2) * 128 : (blk % 2 + 1) * 128]
                        acc = w * v if acc is None else acc + w * v
                    accs.append(acc)
            a = [accs[i] for i in (0, 4, 2, 6, 1, 5, 3, 7)]
            a = [merge(a[i], a[i + 1], 4, m4) for i in (0, 2, 4, 6)]
            a = [merge(a[i], a[i + 1], 2, m2) for i in (0, 2)]
            out = merge(a[0], a[1], 1, m1) * jnp.where(m4, info[2 * o][1], info[2 * o + 1][1])
            polar[pl.ds(pl.multiple_of((g * MATES + o % MATES) * 8, 8), 8), :] = out
            send_ref[g, o % MATES] = out.astype(jnp.bfloat16)
            total = total + out

        @pl.when(step == HELD // ROUND - 1)
        def _():
            pl.semaphore_wait(barrier, LEVS + MATES + PLANES - 3)
            for j in range(HELD):
                plane_copy(j).start()

        for r in range(ROUND):
            i = step * ROUND + r

            @pl.when(jnp.logical_and(i >= HELD, i < PLANES - 1))
            def _():
                plane_copy(i).start()

        return total, count

    total, count = lax.fori_loop(0, PLANES // ROUND, regrid, (jnp.zeros((8, 128), jnp.float32), 0.0))
    parts = []
    for b in range(4):
        value = polar[pl.ds(b, OWNERS * SLOTS, stride=4), :]
        for _ in range(3):
            term = value.astype(jnp.bfloat16)
            parts.append(term)
            value = value - term.astype(jnp.float32)
    acc = lax.dot_general(
        mean_ref[...], jnp.concatenate(parts, 1), (((1,), (1,)), ((), ())), preferred_element_type=jnp.float32
    )
    profs[0] = acc
    each(LEVS, lambda d: prof_copy(d).start())
    sums = jnp.where(m4, jnp.where(sub == 1, count, 0.0), total + pltpu.roll(total, 4, 0))
    planes[PLANES - 1] = send_ref[z]

    each(LEVS, lambda d: prof_copy(d).wait_recv())
    whole = jnp.concatenate([profs[lax.rem(lev - l + LEVS, LEVS)] for l in range(LEVS)], 0)
    both = lax.dot_general(
        jnp.concatenate([acc, jnp.ones((8, OWNERS * SLOTS), jnp.float32)], 0), whole, (((1,), (1,)), ((), ())),
        precision=lax.Precision.HIGHEST, preferred_element_type=jnp.float32,
    )
    for c in range(4):
        part[c] = both[c * 8 : (c + 1) * 8]
    part[4] = jnp.where(sub == 0, both[32:40], sums)

    def r1_copy(c):
        d = lax.rem(c - yc + MATES, MATES)
        return copy(part.at[c], red1.at[d], r1_s.at[c], r1_r.at[d], {"tm": z * MATES + c})

    def r2_copy(d):
        return copy(mine.at[0], red2.at[d], r2_s.at[d], r2_r.at[d], plane_peer(d))

    def r3_copy(d):
        return copy(mine.at[1], red3.at[yc], r3_s.at[d], r3_r.at[yc], mate_peer(d))

    def r1_each(f):
        for c in range(CHUNKS):
            @pl.when(yc != c)
            def _():
                f(c)

    def pass_on(g):
        for i in range(g * PER, (g + 1) * PER):
            if i < PLANES - 1:
                plane_copy(i).wait_recv()
        each(MATES, lambda d: mate_copy(g, d).start())

    r1_each(lambda c: r1_copy(c).start())

    @pl.when(yc < CHUNKS)
    def _():
        def arrived(d):
            return copy(part.at[0], red1.at[d], r1_s.at[0], r1_r.at[d], mate_peer(1))

        each(MATES, lambda d: arrived(d).wait_recv())
        red1[0] = part[yc]
        total = red1[lax.rem(yc, MATES)]
        for m in range(1, MATES):
            total += red1[lax.rem(yc - m + MATES, MATES)]
        mine[0] = total
        each(PLANES, lambda i: r2_copy(distance(i - 1)).start())

    pass_on(0)
    pass_on(1)

    @pl.when(yc < CHUNKS)
    def _():
        each(PLANES, lambda d: r2_copy(d).wait_recv())
        red2[0] = mine[0]
        total = red2[lax.rem(z, PLANES)]
        for m in range(1, PLANES):
            total += red2[lax.rem(z - m + PLANES, PLANES)]
        mine[1] = total
        red3[yc] = total
        each(MATES, lambda d: r3_copy(d).start())

    pass_on(2)
    pass_on(3)

    lane = lax.broadcasted_iota(jnp.int32, (8, 128), 1)
    ids = jnp.zeros((8, 128), jnp.float32)
    for d in range(PLANES):
        ids = jnp.where(lane // 8 == d, planes[d, MATES].astype(jnp.float32), ids)
    names[...] = ids
    each(MATES, lambda d: name_copy(d).start())

    for c in range(CHUNKS):
        @pl.when(yc != c)
        def _():
            copy(mine.at[1], red3.at[c], r3_s.at[0], r3_r.at[c], mate_peer(1)).wait_recv()

    loads[9].wait()
    count = red3[4, 1:2, :]
    every = red3[4, 0:1, :] / count
    row = lax.broadcasted_iota(jnp.int32, (NR, 128), 0)
    column = lax.broadcasted_iota(jnp.int32, (NR, 128), 1)
    own = jnp.sum(jnp.where(column == lev * NR + row, every, 0.0), axis=1, keepdims=True)
    gram = jnp.concatenate([red3[c] for c in range(4)], 0)
    cov_ref[...] = gram / count - own * every
    comp = red3[4, 4:8, :] / count
    comp = jnp.concatenate([comp[b : b + 1] for b in range(4)], 1)
    high = comp.astype(jnp.bfloat16).astype(jnp.float32)
    middle = (comp - high).astype(jnp.bfloat16).astype(jnp.float32)
    terms = jnp.concatenate([high, middle, comp - high - middle], 0).astype(jnp.bfloat16)
    terms = jnp.dot(terms, unsort_ref[...], preferred_element_type=jnp.float32)
    comp_ref[...] = terms[0:1] + terms[1:2] + terms[2:3]

    named[0] = names[...]
    mates[0] = planes[:, yc]
    line = lax.broadcasted_iota(jnp.int32, (128, 128), 0)
    lane = lax.broadcasted_iota(jnp.int32, (128, 128), 1)
    wanted = jnp.where(lane % 4 == line // POINTS_DEV, line % POINTS_DEV, -9).astype(jnp.float32)
    each(MATES, lambda d: name_copy(d).wait_recv())
    picked = jnp.zeros((128, 128), jnp.float32)
    for g in range(GROUPS):
        each(MATES, lambda d: mate_copy(g, d).wait_recv())
    for d in range(MATES):
        hit = jnp.where(wanted == named[d, pl.ds(yc, 1), :], 1.0, 0.0).astype(jnp.bfloat16)
        rows = mates[d].astype(jnp.float32).reshape(128, 128).astype(jnp.bfloat16)
        picked += jnp.dot(hit, rows, preferred_element_type=jnp.float32)
    wide = jnp.concatenate([picked[b * POINTS_DEV : (b + 1) * POINTS_DEV] for b in range(4)], 1).astype(jnp.bfloat16)
    out_ref[...] = jnp.dot(wide, unsort_ref[...], preferred_element_type=jnp.float32).astype(jnp.bfloat16)

    each(LEVS, lambda d: prof_copy(d).wait_send())
    each(PLANES, lambda i: plane_copy(i - 1).wait_send())
    each(MATES, lambda d: name_copy(d).wait_send())
    for g in range(GROUPS):
        each(MATES, lambda d: mate_copy(g, d).wait_send())
    r1_each(lambda c: r1_copy(c).wait_send())

    @pl.when(yc < CHUNKS)
    def _():
        each(PLANES, lambda d: r2_copy(d).wait_send())
        each(MATES, lambda d: r3_copy(d).wait_send())


def finish_kernel(out_in, comp_in, cov_in, out_ref, comp_ref, cov_ref):
    out_ref[...] = out_in[...]
    comp_ref[...] = comp_in[...]
    cov_ref[...] = cov_in[...]


def body(field, patch_list, track_time, track_row, track_col):
    stretch, weights, across, mean, unsort = tables()
    smem, vmem, dma = pltpu.SMEM, pltpu.VMEM, pltpu.SemaphoreType.DMA
    i32, f32, bf16 = jnp.int32, jnp.float32, jnp.bfloat16
    out, comp, cov = pl.pallas_call(
        kernel,
        out_shape=(
            jax.ShapeDtypeStruct((POINTS_DEV, NR * NA), bf16),
            jax.ShapeDtypeStruct((1, NR * NA), f32),
            jax.ShapeDtypeStruct((NR, 128), f32),
        ),
        in_specs=[pl.BlockSpec(memory_space=pl.ANY)] * 10,
        out_specs=(pl.BlockSpec(memory_space=vmem),) * 3,
        scratch_shapes=[
            vmem(field.shape, bf16), smem((SLOTS, OWNERS), i32),
            smem(track_time.shape, i32), smem(track_row.shape, i32), smem(track_col.shape, i32),
            smem(stretch.shape, f32), vmem(weights.shape, bf16), vmem(across.shape, f32), vmem(mean.shape, bf16),
            vmem(unsort.shape, bf16), dma((10,)),
            vmem((2, 3, SIZE, 128), f32), vmem((OWNERS * 8, 128), f32), vmem((PLANES, MATES + 1, 8, 128), bf16),
            vmem((PLANES, MATES + 1, 8, 128), bf16), vmem((MATES, PLANES, 8, 128), bf16),
            vmem((8, 128), f32), vmem((MATES, 8, 128), f32), vmem((LEVS, NR, OWNERS * SLOTS), f32),
            vmem((CHUNKS, 8, 128), f32), vmem((MATES, 8, 128), f32), vmem((PLANES, 8, 128), f32),
            vmem((MATES, 8, 128), f32), vmem((2, 8, 128), f32),
            dma((PLANES,)), dma((PLANES,)), dma((GROUPS, MATES)), dma((GROUPS, MATES)), dma((MATES,)), dma((MATES,)),
            dma((LEVS,)), dma((LEVS,)), dma((MATES,)), dma((MATES,)), dma((PLANES,)), dma((PLANES,)),
            dma((MATES,)), dma((MATES,)),
        ],
        compiler_params=pltpu.CompilerParams(collective_id=0, has_side_effects=True, vmem_limit_bytes=60 << 20),
        name="composites",
    )(
        field, patch_list[0].T, track_time, track_row, track_col,
        jnp.asarray(stretch), jnp.asarray(weights), jnp.asarray(across), jnp.asarray(mean), jnp.asarray(unsort),
    )
    out, comp, cov = pl.pallas_call(
        finish_kernel,
        out_shape=tuple(jax.ShapeDtypeStruct(a.shape, a.dtype) for a in (out, comp, cov)),
        in_specs=[pl.BlockSpec(memory_space=vmem)] * 3,
        out_specs=(pl.BlockSpec(memory_space=vmem),) * 3,
        name="finish",
    )(out, comp, cov)
    return out[:, None, :], comp, cov


def solution(mesh):
    return jax.shard_map(
        body,
        mesh=mesh,
        in_specs=(P("tm", "lev", None, None), P("tm", None, None), P(), P(), P()),
        out_specs=(P("tm", "lev", None), P("lev", None), P("lev", None)),
        check_vma=False,
    )
```

```python
import functools
import math

import jax
import jax.numpy as jnp
import numpy as np
from jax import lax
from jax.experimental import pallas as pl
from jax.experimental.pallas import tpu as pltpu
from jax.sharding import PartitionSpec as P

PATCH, NR, NA = 128, 32, 16
HALF = PATCH // 2
SIZE = 384
POINTS_DEV = 32
OWNERS, SLOTS = 128, 2
PLANES, MATES, LEVS = 16, 8, 4
SPAN = 56
TILES = ((0, 5), (4, 7), (0, 2), (1, 7))
REACH = (48, 1)
GROUPS = 4
CHUNKS = 5
ROUND = 4
HELD = 8


def tables():
    with jax.ensure_compile_time_eval():
        cycle = jnp.arange(NR, dtype=jnp.float32)
        turn = jnp.arange(NA, dtype=jnp.float32)
        radius = (cycle[:, None] + 1.0) * (5.0 * PATCH / (16.0 * NR))
        theta = turn[None, :] * (2.0 * math.pi / NA)
        across = np.asarray((radius * jnp.cos(theta)).reshape(-1))
        along = (radius * jnp.sin(theta)).reshape(-1)
        pos = 0.5 * PATCH + along
        low = jnp.floor(pos)
        frac = pos - low
        upper = np.asarray(frac.astype(jnp.bfloat16)).astype(np.float32)
        lower = np.asarray((1.0 - frac).astype(jnp.bfloat16)).astype(np.float32)
        low = np.asarray(low.astype(jnp.int32))
        latitude = 0.25 * (0.5 * (SIZE - 1) - jnp.arange(SIZE, dtype=jnp.float32))
        stretch = np.asarray(1.0 / jnp.cos(latitude * (math.pi / 180.0)))
    turns = np.arange(NR * NA) % NA
    key = np.where(turns == NA // 4, -1e-3, np.where(turns == 3 * NA // 4, 1e-3, across))
    order = np.argsort(key, kind="stable")
    q = np.arange(NR * NA)
    weights = np.zeros((PATCH, NR * NA), np.float32)
    weights[low[order], q] += lower[order]
    weights[low[order] + 1, q] += upper[order]
    mean = np.zeros((NR, 4, 3, 128), np.float32)
    mean[order // NA, q // 128, :, q % 128] = 1.0 / NA
    mean = mean.reshape(NR, -1).astype(jnp.bfloat16)
    unsort = np.zeros((NR * NA, NR * NA), np.float32)
    unsort[q, order] = 1.0
    spread = np.ascontiguousarray(np.broadcast_to(across[order].reshape(4, 1, 128), (4, 8, 128)), np.float32)
    return stretch, weights.astype(jnp.bfloat16), spread, mean, unsort.astype(jnp.bfloat16)


def merge(a, b, step, mask):
    if step == 4:
        return jnp.where(mask, a, b) + pltpu.roll(jnp.where(mask, b, a), 4, 0)
    return jnp.where(mask, a + pltpu.roll(a, 8 - step, 0), b + pltpu.roll(b, step, 0))


def kernel(
    field_hbm, list_hbm, time_hbm, row_hbm, col_hbm, stretch_hbm, weights_hbm, across_hbm, mean_hbm, unsort_hbm,
    out_ref, comp_ref, cov_ref,
    field_ref, list_ref, time_ref, row_ref, col_ref, stretch_ref, weights_ref, across_ref, mean_ref, unsort_ref, load_s,
    turned, polar, send_ref,
    planes, mates, names, named, profs, part, red1, red2, red3, mine,
    plane_s, plane_r, mate_s, mate_r, name_s, name_r, prof_s, prof_r, r1_s, r1_r, r2_s, r2_r, r3_s, r3_r,
):
    tm, lev = lax.axis_index("tm"), lax.axis_index("lev")
    z, yc = tm // MATES, lax.rem(tm, MATES)
    PER = PLANES // GROUPS

    def distance(i):
        half = (i + 1) // 2
        return lax.rem(PLANES // 2 + jnp.where(lax.rem(i, 2) == 1, half, -half), PLANES)

    def plane_peer(d):
        return {"tm": lax.rem(z + d, PLANES) * MATES + yc}

    def mate_peer(d):
        return {"tm": z * MATES + lax.rem(yc + d, MATES)}

    def lev_peer(d):
        return {"lev": lax.rem(lev + d, LEVS)}

    def copy(src, dst, s, r, peer):
        return pltpu.make_async_remote_copy(
            src_ref=src, dst_ref=dst, send_sem=s, recv_sem=r, device_id=peer, device_id_type=pl.DeviceIdType.MESH
        )

    def each(n, f):
        def step(i, c):
            f(i)
            return c

        lax.fori_loop(1, n, step, 0)

    barrier = pltpu.get_barrier_semaphore()

    def greet(peer):
        pl.semaphore_signal(barrier, inc=1, device_id=peer, device_id_type=pl.DeviceIdType.MESH)

    loads = [
        pltpu.make_async_copy(src, dst, load_s.at[i])
        for i, (src, dst) in enumerate((
            (field_hbm, field_ref), (list_hbm, list_ref), (time_hbm, time_ref), (row_hbm, row_ref), (col_hbm, col_ref),
            (stretch_hbm, stretch_ref), (weights_hbm, weights_ref), (across_hbm, across_ref), (mean_hbm, mean_ref),
            (unsort_hbm, unsort_ref),
        ))
    ]
    for load in loads:
        load.start()
    each(PLANES, lambda i: greet(plane_peer(distance(i - 1))))
    each(LEVS, lambda d: greet(lev_peer(d)))
    each(MATES, lambda d: greet(mate_peer(d)))


    def prof_copy(d):
        return copy(profs.at[0], profs.at[d], prof_s.at[d], prof_r.at[d], lev_peer(d))

    def plane_copy(i):
        d = distance(i)
        there = lax.rem(z + d, PLANES)
        return copy(send_ref.at[there], planes.at[i], plane_s.at[i], plane_r.at[i], plane_peer(d))

    def mate_copy(g, d):
        there = lax.rem(yc + d, MATES)
        return copy(
            planes.at[pl.ds(g * PER, PER), there], mates.at[d, pl.ds(g * PER, PER)],
            mate_s.at[g, d], mate_r.at[g, d], mate_peer(d),
        )

    def name_copy(d):
        return copy(names, named.at[d], name_s.at[d], name_r.at[d], mate_peer(d))

    loads[0].wait()
    for t in range(2):
        for i in range(3):
            for j in range(3):
                tile = field_ref[t, 0, i * 128 : (i + 1) * 128, j * 128 : (j + 1) * 128]
                turned[t, i, j * 128 : (j + 1) * 128, :] = tile.astype(jnp.float32).T
    for load in loads[1:9]:
        load.wait()
    sub = lax.broadcasted_iota(jnp.int32, (8, 128), 0)
    first = (lax.broadcasted_iota(jnp.int32, (8, 128), 1) & 4) == 0
    lane = lax.broadcasted_iota(jnp.int32, (SPAN, 128), 1)
    from_start = [reach - sub.astype(jnp.float32) for reach in REACH]
    m4, m2, m1 = sub < 4, (sub & 2) == 0, (sub & 1) == 0


    def regrid(step, carry):
        total, count = carry
        halves, info = ([], []), []
        planes_now = [lax.rem(z + distance(step * ROUND + r), PLANES) for r in range(ROUND)]
        for g in planes_now:
            points = jnp.zeros((8, 128), jnp.int32)
            for o in range(MATES):
                owner = g * MATES + o
                ids = [list_ref[p, owner] for p in range(SLOTS)]
                for k in ids:
                    point = owner * POINTS_DEV + jnp.maximum(k, 0)
                    t = jnp.clip(time_ref[point] - 2 * tm, 0, 1)
                    row = jnp.clip(row_ref[point], HALF, SIZE - HALF)
                    col = jnp.clip(col_ref[point], HALF, SIZE - HALF)
                    top = row - HALF
                    b = jnp.minimum(top // 128, 1)
                    off = top - b * 128
                    for h in range(2):
                        start = col - REACH[h]
                        one = turned[t, b, pl.ds(start, SPAN), :]
                        two = turned[t, b + 1, pl.ds(start, SPAN), :]
                        halves[h].append(pltpu.roll(jnp.where(lane >= off, one, two), 128 - off, 1))
                    live = jnp.where(k >= 0, 1.0, 0.0)
                    count += live
                    info.append((stretch_ref[row], live))
                points = jnp.where(sub == o, jnp.where(first, ids[0], ids[1]), points)
            send_ref[g, MATES] = points.astype(jnp.float32).astype(jnp.bfloat16)
        mixed = [
            jnp.dot(
                jnp.concatenate(halves[h], 0).astype(jnp.bfloat16),
                weights_ref[:, h * 256 : (h + 1) * 256],
                preferred_element_type=jnp.float32,
            )
            for h in range(2)
        ]
        for o in range(ROUND * MATES):
            g = planes_now[o // MATES]
            accs = []
            for n in (2 * o, 2 * o + 1):
                for blk in range(4):
                    base = across_ref[blk] * info[n][0] + from_start[blk // 2]
                    acc = None
                    for tile in range(*TILES[blk]):
                        w = jnp.maximum(1.0 - jnp.abs(base - 8.0 * tile), 0.0)
                        at = n * SPAN + tile * 8
                        v = mixed[blk // 2][at : at + 8, (blk % 2) * 128 : (blk % 2 + 1) * 128]
                        acc = w * v if acc is None else acc + w * v
                    accs.append(acc)
            a = [accs[i] for i in (0, 4, 2, 6, 1, 5, 3, 7)]
            a = [merge(a[i], a[i + 1], 4, m4) for i in (0, 2, 4, 6)]
            a = [merge(a[i], a[i + 1], 2, m2) for i in (0, 2)]
            out = merge(a[0], a[1], 1, m1) * jnp.where(m4, info[2 * o][1], info[2 * o + 1][1])
            polar[pl.ds(pl.multiple_of((g * MATES + o % MATES) * 8, 8), 8), :] = out
            send_ref[g, o % MATES] = out.astype(jnp.bfloat16)
            total = total + out

        @pl.when(step == HELD // ROUND - 1)
        def _():
            pl.semaphore_wait(barrier, LEVS + MATES + PLANES - 3)
            for j in range(HELD):
                plane_copy(j).start()

        for r in range(ROUND):
            i = step * ROUND + r

            @pl.when(jnp.logical_and(i >= HELD, i < PLANES - 1))
            def _():
                plane_copy(i).start()

        return total, count

    total, count = lax.fori_loop(0, PLANES // ROUND, regrid, (jnp.zeros((8, 128), jnp.float32), 0.0))
    parts = []
    for b in range(4):
        value = polar[pl.ds(b, OWNERS * SLOTS, stride=4), :]
        for _ in range(3):
            term = value.astype(jnp.bfloat16)
            parts.append(term)
            value = value - term.astype(jnp.float32)
    acc = lax.dot_general(
        mean_ref[...], jnp.concatenate(parts, 1), (((1,), (1,)), ((), ())), preferred_element_type=jnp.float32
    )
    profs[0] = acc
    each(LEVS, lambda d: prof_copy(d).start())
    sums = jnp.where(m4, jnp.where(sub == 1, count, 0.0), total + pltpu.roll(total, 4, 0))
    planes[PLANES - 1] = send_ref[z]

    each(LEVS, lambda d: prof_copy(d).wait_recv())
    whole = jnp.concatenate([profs[lax.rem(lev - l + LEVS, LEVS)] for l in range(LEVS)], 0)
    both = lax.dot_general(
        jnp.concatenate([acc, jnp.ones((8, OWNERS * SLOTS), jnp.float32)], 0), whole, (((1,), (1,)), ((), ())),
        precision=lax.Precision.HIGHEST, preferred_element_type=jnp.float32,
    )
    for c in range(4):
        part[c] = both[c * 8 : (c + 1) * 8]
    part[4] = jnp.where(sub == 0, both[32:40], sums)

    def r1_copy(c):
        d = lax.rem(c - yc + MATES, MATES)
        return copy(part.at[c], red1.at[d], r1_s.at[c], r1_r.at[d], {"tm": z * MATES + c})

    def r2_copy(d):
        return copy(mine.at[0], red2.at[d], r2_s.at[d], r2_r.at[d], plane_peer(d))

    def r3_copy(d):
        return copy(mine.at[1], red3.at[yc], r3_s.at[d], r3_r.at[yc], mate_peer(d))

    def r1_each(f):
        for c in range(CHUNKS):
            @pl.when(yc != c)
            def _():
                f(c)

    def pass_on(g):
        for i in range(g * PER, (g + 1) * PER):
            if i < PLANES - 1:
                plane_copy(i).wait_recv()
        each(MATES, lambda d: mate_copy(g, d).start())

    r1_each(lambda c: r1_copy(c).start())

    @pl.when(yc < CHUNKS)
    def _():
        def arrived(d):
            return copy(part.at[0], red1.at[d], r1_s.at[0], r1_r.at[d], mate_peer(1))

        each(MATES, lambda d: arrived(d).wait_recv())
        red1[0] = part[yc]
        total = red1[lax.rem(yc, MATES)]
        for m in range(1, MATES):
            total += red1[lax.rem(yc - m + MATES, MATES)]
        mine[0] = total
        each(PLANES, lambda i: r2_copy(distance(i - 1)).start())

    pass_on(0)
    pass_on(1)

    pass_on(2)
    pass_on(3)

    lane = lax.broadcasted_iota(jnp.int32, (8, 128), 1)
    ids = jnp.zeros((8, 128), jnp.float32)
    for d in range(PLANES):
        ids = jnp.where(lane // 8 == d, planes[d, MATES].astype(jnp.float32), ids)
    names[...] = ids
    each(MATES, lambda d: name_copy(d).start())

    @pl.when(yc < CHUNKS)
    def _():
        each(PLANES, lambda d: r2_copy(d).wait_recv())
        red2[0] = mine[0]
        total = red2[lax.rem(z, PLANES)]
        for m in range(1, PLANES):
            total += red2[lax.rem(z - m + PLANES, PLANES)]
        mine[1] = total
        red3[yc] = total
        each(MATES, lambda d: r3_copy(d).start())

    named[0] = names[...]
    mates[0] = planes[:, yc]
    line = lax.broadcasted_iota(jnp.int32, (128, 128), 0)
    lane = lax.broadcasted_iota(jnp.int32, (128, 128), 1)
    wanted = jnp.where(lane % 4 == line // POINTS_DEV, line % POINTS_DEV, -9).astype(jnp.float32)
    each(MATES, lambda d: name_copy(d).wait_recv())
    picked = jnp.zeros((128, 128), jnp.float32)
    for g in range(GROUPS):
        each(MATES, lambda d: mate_copy(g, d).wait_recv())
    for d in range(MATES):
        hit = jnp.where(wanted == named[d, pl.ds(yc, 1), :], 1.0, 0.0).astype(jnp.bfloat16)
        rows = mates[d].astype(jnp.float32).reshape(128, 128).astype(jnp.bfloat16)
        picked += jnp.dot(hit, rows, preferred_element_type=jnp.float32)
    wide = jnp.concatenate([picked[b * POINTS_DEV : (b + 1) * POINTS_DEV] for b in range(4)], 1).astype(jnp.bfloat16)
    loads[9].wait()
    out_ref[...] = jnp.dot(wide, unsort_ref[...], preferred_element_type=jnp.float32).astype(jnp.bfloat16)

    for c in range(CHUNKS):
        @pl.when(yc != c)
        def _():
            copy(mine.at[1], red3.at[c], r3_s.at[0], r3_r.at[c], mate_peer(1)).wait_recv()

    count = red3[4, 1:2, :]
    every = red3[4, 0:1, :] / count
    row = lax.broadcasted_iota(jnp.int32, (NR, 128), 0)
    column = lax.broadcasted_iota(jnp.int32, (NR, 128), 1)
    own = jnp.sum(jnp.where(column == lev * NR + row, every, 0.0), axis=1, keepdims=True)
    gram = jnp.concatenate([red3[c] for c in range(4)], 0)
    cov_ref[...] = gram / count - own * every
    comp = red3[4, 4:8, :] / count
    comp = jnp.concatenate([comp[b : b + 1] for b in range(4)], 1)
    high = comp.astype(jnp.bfloat16).astype(jnp.float32)
    middle = (comp - high).astype(jnp.bfloat16).astype(jnp.float32)
    terms = jnp.concatenate([high, middle, comp - high - middle], 0).astype(jnp.bfloat16)
    terms = jnp.dot(terms, unsort_ref[...], preferred_element_type=jnp.float32)
    comp_ref[...] = terms[0:1] + terms[1:2] + terms[2:3]

    each(LEVS, lambda d: prof_copy(d).wait_send())
    each(PLANES, lambda i: plane_copy(i - 1).wait_send())
    each(MATES, lambda d: name_copy(d).wait_send())
    for g in range(GROUPS):
        each(MATES, lambda d: mate_copy(g, d).wait_send())
    r1_each(lambda c: r1_copy(c).wait_send())

    @pl.when(yc < CHUNKS)
    def _():
        each(PLANES, lambda d: r2_copy(d).wait_send())
        each(MATES, lambda d: r3_copy(d).wait_send())


def finish_kernel(out_in, comp_in, cov_in, out_ref, comp_ref, cov_ref):
    out_ref[...] = out_in[...]
    comp_ref[...] = comp_in[...]
    cov_ref[...] = cov_in[...]


def body(field, patch_list, track_time, track_row, track_col):
    stretch, weights, across, mean, unsort = tables()
    smem, vmem, dma = pltpu.SMEM, pltpu.VMEM, pltpu.SemaphoreType.DMA
    i32, f32, bf16 = jnp.int32, jnp.float32, jnp.bfloat16
    out, comp, cov = pl.pallas_call(
        kernel,
        out_shape=(
            jax.ShapeDtypeStruct((POINTS_DEV, NR * NA), bf16),
            jax.ShapeDtypeStruct((1, NR * NA), f32),
            jax.ShapeDtypeStruct((NR, 128), f32),
        ),
        in_specs=[pl.BlockSpec(memory_space=pl.ANY)] * 10,
        out_specs=(pl.BlockSpec(memory_space=vmem),) * 3,
        scratch_shapes=[
            vmem(field.shape, bf16), smem((SLOTS, OWNERS), i32),
            smem(track_time.shape, i32), smem(track_row.shape, i32), smem(track_col.shape, i32),
            smem(stretch.shape, f32), vmem(weights.shape, bf16), vmem(across.shape, f32), vmem(mean.shape, bf16),
            vmem(unsort.shape, bf16), dma((10,)),
            vmem((2, 3, SIZE, 128), f32), vmem((OWNERS * 8, 128), f32), vmem((PLANES, MATES + 1, 8, 128), bf16),
            vmem((PLANES, MATES + 1, 8, 128), bf16), vmem((MATES, PLANES, 8, 128), bf16),
            vmem((8, 128), f32), vmem((MATES, 8, 128), f32), vmem((LEVS, NR, OWNERS * SLOTS), f32),
            vmem((CHUNKS, 8, 128), f32), vmem((MATES, 8, 128), f32), vmem((PLANES, 8, 128), f32),
            vmem((MATES, 8, 128), f32), vmem((2, 8, 128), f32),
            dma((PLANES,)), dma((PLANES,)), dma((GROUPS, MATES)), dma((GROUPS, MATES)), dma((MATES,)), dma((MATES,)),
            dma((LEVS,)), dma((LEVS,)), dma((MATES,)), dma((MATES,)), dma((PLANES,)), dma((PLANES,)),
            dma((MATES,)), dma((MATES,)),
        ],
        compiler_params=pltpu.CompilerParams(collective_id=0, has_side_effects=True, vmem_limit_bytes=60 << 20),
        name="composites",
    )(
        field, patch_list[0].T, track_time, track_row, track_col,
        jnp.asarray(stretch), jnp.asarray(weights), jnp.asarray(across), jnp.asarray(mean), jnp.asarray(unsort),
    )
    out, comp, cov = pl.pallas_call(
        finish_kernel,
        out_shape=tuple(jax.ShapeDtypeStruct(a.shape, a.dtype) for a in (out, comp, cov)),
        in_specs=[pl.BlockSpec(memory_space=vmem)] * 3,
        out_specs=(pl.BlockSpec(memory_space=vmem),) * 3,
        name="finish",
    )(out, comp, cov)
    return out[:, None, :], comp, cov


def solution(mesh):
    return jax.shard_map(
        body,
        mesh=mesh,
        in_specs=(P("tm", "lev", None, None), P("tm", None, None), P(), P(), P()),
        out_specs=(P("tm", "lev", None), P("lev", None), P("lev", None)),
        check_vma=False,
    )
```

```python
import functools
import math

import jax
import jax.numpy as jnp
import numpy as np
from jax import lax
from jax.experimental import pallas as pl
from jax.experimental.pallas import tpu as pltpu
from jax.sharding import PartitionSpec as P

PATCH, NR, NA = 128, 32, 16
HALF = PATCH // 2
SIZE = 384
POINTS_DEV = 32
OWNERS, SLOTS = 128, 2
PLANES, MATES, LEVS = 16, 8, 4
SPAN = 56
TILES = ((0, 5), (4, 7), (0, 2), (1, 7))
REACH = (48, 1)
GROUPS = 4
CHUNKS = 5
ROUND = 8
HELD = 8


def tables():
    with jax.ensure_compile_time_eval():
        cycle = jnp.arange(NR, dtype=jnp.float32)
        turn = jnp.arange(NA, dtype=jnp.float32)
        radius = (cycle[:, None] + 1.0) * (5.0 * PATCH / (16.0 * NR))
        theta = turn[None, :] * (2.0 * math.pi / NA)
        across = np.asarray((radius * jnp.cos(theta)).reshape(-1))
        along = (radius * jnp.sin(theta)).reshape(-1)
        pos = 0.5 * PATCH + along
        low = jnp.floor(pos)
        frac = pos - low
        upper = np.asarray(frac.astype(jnp.bfloat16)).astype(np.float32)
        lower = np.asarray((1.0 - frac).astype(jnp.bfloat16)).astype(np.float32)
        low = np.asarray(low.astype(jnp.int32))
        latitude = 0.25 * (0.5 * (SIZE - 1) - jnp.arange(SIZE, dtype=jnp.float32))
        stretch = np.asarray(1.0 / jnp.cos(latitude * (math.pi / 180.0)))
    turns = np.arange(NR * NA) % NA
    key = np.where(turns == NA // 4, -1e-3, np.where(turns == 3 * NA // 4, 1e-3, across))
    order = np.argsort(key, kind="stable")
    q = np.arange(NR * NA)
    weights = np.zeros((PATCH, NR * NA), np.float32)
    weights[low[order], q] += lower[order]
    weights[low[order] + 1, q] += upper[order]
    mean = np.zeros((NR, 4, 3, 128), np.float32)
    mean[order // NA, q // 128, :, q % 128] = 1.0 / NA
    mean = mean.reshape(NR, -1).astype(jnp.bfloat16)
    unsort = np.zeros((NR * NA, NR * NA), np.float32)
    unsort[q, order] = 1.0
    spread = np.ascontiguousarray(np.broadcast_to(across[order].reshape(4, 1, 128), (4, 8, 128)), np.float32)
    return stretch, weights.astype(jnp.bfloat16), spread, mean, unsort.astype(jnp.bfloat16)


def merge(a, b, step, mask):
    if step == 4:
        return jnp.where(mask, a, b) + pltpu.roll(jnp.where(mask, b, a), 4, 0)
    return jnp.where(mask, a + pltpu.roll(a, 8 - step, 0), b + pltpu.roll(b, step, 0))


def kernel(
    field_hbm, list_hbm, time_hbm, row_hbm, col_hbm, stretch_hbm, weights_hbm, across_hbm, mean_hbm, unsort_hbm,
    out_ref, comp_ref, cov_ref,
    field_ref, list_ref, time_ref, row_ref, col_ref, stretch_ref, weights_ref, across_ref, mean_ref, unsort_ref, load_s,
    turned, polar, send_ref,
    planes, mates, names, named, profs, part, red1, red2, red3, mine,
    plane_s, plane_r, mate_s, mate_r, name_s, name_r, prof_s, prof_r, r1_s, r1_r, r2_s, r2_r, r3_s, r3_r,
):
    tm, lev = lax.axis_index("tm"), lax.axis_index("lev")
    z, yc = tm // MATES, lax.rem(tm, MATES)
    PER = PLANES // GROUPS

    def distance(i):
        half = (i + 1) // 2
        return lax.rem(PLANES // 2 + jnp.where(lax.rem(i, 2) == 1, half, -half), PLANES)

    def plane_peer(d):
        return {"tm": lax.rem(z + d, PLANES) * MATES + yc}

    def mate_peer(d):
        return {"tm": z * MATES + lax.rem(yc + d, MATES)}

    def lev_peer(d):
        return {"lev": lax.rem(lev + d, LEVS)}

    def copy(src, dst, s, r, peer):
        return pltpu.make_async_remote_copy(
            src_ref=src, dst_ref=dst, send_sem=s, recv_sem=r, device_id=peer, device_id_type=pl.DeviceIdType.MESH
        )

    def each(n, f):
        def step(i, c):
            f(i)
            return c

        lax.fori_loop(1, n, step, 0)

    barrier = pltpu.get_barrier_semaphore()

    def greet(peer):
        pl.semaphore_signal(barrier, inc=1, device_id=peer, device_id_type=pl.DeviceIdType.MESH)

    loads = [
        pltpu.make_async_copy(src, dst, load_s.at[i])
        for i, (src, dst) in enumerate((
            (field_hbm, field_ref), (list_hbm, list_ref), (time_hbm, time_ref), (row_hbm, row_ref), (col_hbm, col_ref),
            (stretch_hbm, stretch_ref), (weights_hbm, weights_ref), (across_hbm, across_ref), (mean_hbm, mean_ref),
            (unsort_hbm, unsort_ref),
        ))
    ]
    for load in loads:
        load.start()
    each(PLANES, lambda i: greet(plane_peer(distance(i - 1))))
    each(LEVS, lambda d: greet(lev_peer(d)))
    each(MATES, lambda d: greet(mate_peer(d)))


    def prof_copy(d):
        return copy(profs.at[0], profs.at[d], prof_s.at[d], prof_r.at[d], lev_peer(d))

    def plane_copy(i):
        d = distance(i)
        there = lax.rem(z + d, PLANES)
        return copy(send_ref.at[there], planes.at[i], plane_s.at[i], plane_r.at[i], plane_peer(d))

    def mate_copy(g, d):
        there = lax.rem(yc + d, MATES)
        return copy(
            planes.at[pl.ds(g * PER, PER), there], mates.at[d, pl.ds(g * PER, PER)],
            mate_s.at[g, d], mate_r.at[g, d], mate_peer(d),
        )

    def name_copy(d):
        return copy(names, named.at[d], name_s.at[d], name_r.at[d], mate_peer(d))

    loads[0].wait()
    for t in range(2):
        for i in range(3):
            for j in range(3):
                tile = field_ref[t, 0, i * 128 : (i + 1) * 128, j * 128 : (j + 1) * 128]
                turned[t, i, j * 128 : (j + 1) * 128, :] = tile.astype(jnp.float32).T
    for load in loads[1:9]:
        load.wait()
    sub = lax.broadcasted_iota(jnp.int32, (8, 128), 0)
    first = (lax.broadcasted_iota(jnp.int32, (8, 128), 1) & 4) == 0
    lane = lax.broadcasted_iota(jnp.int32, (SPAN, 128), 1)
    from_start = [reach - sub.astype(jnp.float32) for reach in REACH]
    m4, m2, m1 = sub < 4, (sub & 2) == 0, (sub & 1) == 0


    def regrid(step, carry):
        total, count = carry
        halves, info = ([], []), []
        planes_now = [lax.rem(z + distance(step * ROUND + r), PLANES) for r in range(ROUND)]
        for g in planes_now:
            points = jnp.zeros((8, 128), jnp.int32)
            for o in range(MATES):
                owner = g * MATES + o
                ids = [list_ref[p, owner] for p in range(SLOTS)]
                for k in ids:
                    point = owner * POINTS_DEV + jnp.maximum(k, 0)
                    t = jnp.clip(time_ref[point] - 2 * tm, 0, 1)
                    row = jnp.clip(row_ref[point], HALF, SIZE - HALF)
                    col = jnp.clip(col_ref[point], HALF, SIZE - HALF)
                    top = row - HALF
                    b = jnp.minimum(top // 128, 1)
                    off = top - b * 128
                    for h in range(2):
                        start = col - REACH[h]
                        one = turned[t, b, pl.ds(start, SPAN), :]
                        two = turned[t, b + 1, pl.ds(start, SPAN), :]
                        halves[h].append(pltpu.roll(jnp.where(lane >= off, one, two), 128 - off, 1))
                    live = jnp.where(k >= 0, 1.0, 0.0)
                    count += live
                    info.append((stretch_ref[row], live))
                points = jnp.where(sub == o, jnp.where(first, ids[0], ids[1]), points)
            send_ref[g, MATES] = points.astype(jnp.float32).astype(jnp.bfloat16)
        mixed = [
            jnp.dot(
                jnp.concatenate(halves[h], 0).astype(jnp.bfloat16),
                weights_ref[:, h * 256 : (h + 1) * 256],
                preferred_element_type=jnp.float32,
            )
            for h in range(2)
        ]
        for o in range(ROUND * MATES):
            g = planes_now[o // MATES]
            accs = []
            for n in (2 * o, 2 * o + 1):
                for blk in range(4):
                    base = across_ref[blk] * info[n][0] + from_start[blk // 2]
                    acc = None
                    for tile in range(*TILES[blk]):
                        w = jnp.maximum(1.0 - jnp.abs(base - 8.0 * tile), 0.0)
                        at = n * SPAN + tile * 8
                        v = mixed[blk // 2][at : at + 8, (blk % 2) * 128 : (blk % 2 + 1) * 128]
                        acc = w * v if acc is None else acc + w * v
                    accs.append(acc)
            a = [accs[i] for i in (0, 4, 2, 6, 1, 5, 3, 7)]
            a = [merge(a[i], a[i + 1], 4, m4) for i in (0, 2, 4, 6)]
            a = [merge(a[i], a[i + 1], 2, m2) for i in (0, 2)]
            out = merge(a[0], a[1], 1, m1) * jnp.where(m4, info[2 * o][1], info[2 * o + 1][1])
            polar[pl.ds(pl.multiple_of((g * MATES + o % MATES) * 8, 8), 8), :] = out
            send_ref[g, o % MATES] = out.astype(jnp.bfloat16)
            total = total + out

        @pl.when(step == HELD // ROUND - 1)
        def _():
            pl.semaphore_wait(barrier, LEVS + MATES + PLANES - 3)
            for j in range(HELD):
                plane_copy(j).start()

        for r in range(ROUND):
            i = step * ROUND + r

            @pl.when(jnp.logical_and(i >= HELD, i < PLANES - 1))
            def _():
                plane_copy(i).start()

        return total, count

    total, count = lax.fori_loop(0, PLANES // ROUND, regrid, (jnp.zeros((8, 128), jnp.float32), 0.0))
    parts = []
    for b in range(4):
        value = polar[pl.ds(b, OWNERS * SLOTS, stride=4), :]
        for _ in range(3):
            term = value.astype(jnp.bfloat16)
            parts.append(term)
            value = value - term.astype(jnp.float32)
    acc = lax.dot_general(
        mean_ref[...], jnp.concatenate(parts, 1), (((1,), (1,)), ((), ())), preferred_element_type=jnp.float32
    )
    profs[0] = acc
    each(LEVS, lambda d: prof_copy(d).start())
    sums = jnp.where(m4, jnp.where(sub == 1, count, 0.0), total + pltpu.roll(total, 4, 0))
    planes[PLANES - 1] = send_ref[z]

    each(LEVS, lambda d: prof_copy(d).wait_recv())
    whole = jnp.concatenate([profs[lax.rem(lev - l + LEVS, LEVS)] for l in range(LEVS)], 0)
    both = lax.dot_general(
        jnp.concatenate([acc, jnp.ones((8, OWNERS * SLOTS), jnp.float32)], 0), whole, (((1,), (1,)), ((), ())),
        precision=lax.Precision.HIGHEST, preferred_element_type=jnp.float32,
    )
    for c in range(4):
        part[c] = both[c * 8 : (c + 1) * 8]
    part[4] = jnp.where(sub == 0, both[32:40], sums)

    def r1_copy(c):
        d = lax.rem(c - yc + MATES, MATES)
        return copy(part.at[c], red1.at[d], r1_s.at[c], r1_r.at[d], {"tm": z * MATES + c})

    def r2_copy(d):
        return copy(mine.at[0], red2.at[d], r2_s.at[d], r2_r.at[d], plane_peer(d))

    def r3_copy(d):
        return copy(mine.at[1], red3.at[yc], r3_s.at[d], r3_r.at[yc], mate_peer(d))

    def r1_each(f):
        for c in range(CHUNKS):
            @pl.when(yc != c)
            def _():
                f(c)

    def pass_on(g):
        for i in range(g * PER, (g + 1) * PER):
            if i < PLANES - 1:
                plane_copy(i).wait_recv()
        each(MATES, lambda d: mate_copy(g, d).start())

    r1_each(lambda c: r1_copy(c).start())

    @pl.when(yc < CHUNKS)
    def _():
        def arrived(d):
            return copy(part.at[0], red1.at[d], r1_s.at[0], r1_r.at[d], mate_peer(1))

        each(MATES, lambda d: arrived(d).wait_recv())
        red1[0] = part[yc]
        total = red1[lax.rem(yc, MATES)]
        for m in range(1, MATES):
            total += red1[lax.rem(yc - m + MATES, MATES)]
        mine[0] = total
        each(PLANES, lambda i: r2_copy(distance(i - 1)).start())

    pass_on(0)
    pass_on(1)

    pass_on(2)
    pass_on(3)

    lane = lax.broadcasted_iota(jnp.int32, (8, 128), 1)
    ids = jnp.zeros((8, 128), jnp.float32)
    for d in range(PLANES):
        ids = jnp.where(lane // 8 == d, planes[d, MATES].astype(jnp.float32), ids)
    names[...] = ids
    each(MATES, lambda d: name_copy(d).start())

    @pl.when(yc < CHUNKS)
    def _():
        each(PLANES, lambda d: r2_copy(d).wait_recv())
        red2[0] = mine[0]
        total = red2[lax.rem(z, PLANES)]
        for m in range(1, PLANES):
            total += red2[lax.rem(z - m + PLANES, PLANES)]
        mine[1] = total
        red3[yc] = total
        each(MATES, lambda d: r3_copy(d).start())

    named[0] = names[...]
    mates[0] = planes[:, yc]
    line = lax.broadcasted_iota(jnp.int32, (128, 128), 0)
    lane = lax.broadcasted_iota(jnp.int32, (128, 128), 1)
    wanted = jnp.where(lane % 4 == line // POINTS_DEV, line % POINTS_DEV, -9).astype(jnp.float32)
    each(MATES, lambda d: name_copy(d).wait_recv())
    picked = jnp.zeros((128, 128), jnp.float32)
    for g in range(GROUPS):
        each(MATES, lambda d: mate_copy(g, d).wait_recv())
    for d in range(MATES):
        hit = jnp.where(wanted == named[d, pl.ds(yc, 1), :], 1.0, 0.0).astype(jnp.bfloat16)
        rows = mates[d].astype(jnp.float32).reshape(128, 128).astype(jnp.bfloat16)
        picked += jnp.dot(hit, rows, preferred_element_type=jnp.float32)
    wide = jnp.concatenate([picked[b * POINTS_DEV : (b + 1) * POINTS_DEV] for b in range(4)], 1).astype(jnp.bfloat16)
    loads[9].wait()
    out_ref[...] = jnp.dot(wide, unsort_ref[...], preferred_element_type=jnp.float32).astype(jnp.bfloat16)

    for c in range(CHUNKS):
        @pl.when(yc != c)
        def _():
            copy(mine.at[1], red3.at[c], r3_s.at[0], r3_r.at[c], mate_peer(1)).wait_recv()

    count = red3[4, 1:2, :]
    every = red3[4, 0:1, :] / count
    row = lax.broadcasted_iota(jnp.int32, (NR, 128), 0)
    column = lax.broadcasted_iota(jnp.int32, (NR, 128), 1)
    own = jnp.sum(jnp.where(column == lev * NR + row, every, 0.0), axis=1, keepdims=True)
    gram = jnp.concatenate([red3[c] for c in range(4)], 0)
    cov_ref[...] = gram / count - own * every
    comp = red3[4, 4:8, :] / count
    comp = jnp.concatenate([comp[b : b + 1] for b in range(4)], 1)
    high = comp.astype(jnp.bfloat16).astype(jnp.float32)
    middle = (comp - high).astype(jnp.bfloat16).astype(jnp.float32)
    terms = jnp.concatenate([high, middle, comp - high - middle], 0).astype(jnp.bfloat16)
    terms = jnp.dot(terms, unsort_ref[...], preferred_element_type=jnp.float32)
    comp_ref[...] = terms[0:1] + terms[1:2] + terms[2:3]

    each(LEVS, lambda d: prof_copy(d).wait_send())
    each(PLANES, lambda i: plane_copy(i - 1).wait_send())
    each(MATES, lambda d: name_copy(d).wait_send())
    for g in range(GROUPS):
        each(MATES, lambda d: mate_copy(g, d).wait_send())
    r1_each(lambda c: r1_copy(c).wait_send())

    @pl.when(yc < CHUNKS)
    def _():
        each(PLANES, lambda d: r2_copy(d).wait_send())
        each(MATES, lambda d: r3_copy(d).wait_send())


def finish_kernel(out_in, comp_in, cov_in, out_ref, comp_ref, cov_ref):
    out_ref[...] = out_in[...]
    comp_ref[...] = comp_in[...]
    cov_ref[...] = cov_in[...]


def body(field, patch_list, track_time, track_row, track_col):
    stretch, weights, across, mean, unsort = tables()
    smem, vmem, dma = pltpu.SMEM, pltpu.VMEM, pltpu.SemaphoreType.DMA
    i32, f32, bf16 = jnp.int32, jnp.float32, jnp.bfloat16
    out, comp, cov = pl.pallas_call(
        kernel,
        out_shape=(
            jax.ShapeDtypeStruct((POINTS_DEV, NR * NA), bf16),
            jax.ShapeDtypeStruct((1, NR * NA), f32),
            jax.ShapeDtypeStruct((NR, 128), f32),
        ),
        in_specs=[pl.BlockSpec(memory_space=pl.ANY)] * 10,
        out_specs=(pl.BlockSpec(memory_space=vmem),) * 3,
        scratch_shapes=[
            vmem(field.shape, bf16), smem((SLOTS, OWNERS), i32),
            smem(track_time.shape, i32), smem(track_row.shape, i32), smem(track_col.shape, i32),
            smem(stretch.shape, f32), vmem(weights.shape, bf16), vmem(across.shape, f32), vmem(mean.shape, bf16),
            vmem(unsort.shape, bf16), dma((10,)),
            vmem((2, 3, SIZE, 128), f32), vmem((OWNERS * 8, 128), f32), vmem((PLANES, MATES + 1, 8, 128), bf16),
            vmem((PLANES, MATES + 1, 8, 128), bf16), vmem((MATES, PLANES, 8, 128), bf16),
            vmem((8, 128), f32), vmem((MATES, 8, 128), f32), vmem((LEVS, NR, OWNERS * SLOTS), f32),
            vmem((CHUNKS, 8, 128), f32), vmem((MATES, 8, 128), f32), vmem((PLANES, 8, 128), f32),
            vmem((MATES, 8, 128), f32), vmem((2, 8, 128), f32),
            dma((PLANES,)), dma((PLANES,)), dma((GROUPS, MATES)), dma((GROUPS, MATES)), dma((MATES,)), dma((MATES,)),
            dma((LEVS,)), dma((LEVS,)), dma((MATES,)), dma((MATES,)), dma((PLANES,)), dma((PLANES,)),
            dma((MATES,)), dma((MATES,)),
        ],
        compiler_params=pltpu.CompilerParams(collective_id=0, has_side_effects=True, vmem_limit_bytes=60 << 20),
        name="composites",
    )(
        field, patch_list[0].T, track_time, track_row, track_col,
        jnp.asarray(stretch), jnp.asarray(weights), jnp.asarray(across), jnp.asarray(mean), jnp.asarray(unsort),
    )
    out, comp, cov = pl.pallas_call(
        finish_kernel,
        out_shape=tuple(jax.ShapeDtypeStruct(a.shape, a.dtype) for a in (out, comp, cov)),
        in_specs=[pl.BlockSpec(memory_space=vmem)] * 3,
        out_specs=(pl.BlockSpec(memory_space=vmem),) * 3,
        name="finish",
    )(out, comp, cov)
    return out[:, None, :], comp, cov


def solution(mesh):
    return jax.shard_map(
        body,
        mesh=mesh,
        in_specs=(P("tm", "lev", None, None), P("tm", None, None), P(), P(), P()),
        out_specs=(P("tm", "lev", None), P("lev", None), P("lev", None)),
        check_vma=False,
    )
```
